128 devices in a mesh: gx: 4 (over z_hi, core), gy: 4 (over y), gz: 8 (over z_lo, x).
Axes of the slice: x: 4, y: 4, z: 4 (z_hi: 2, z_lo: 2; z = z_hi * 2 + z_lo), core: 2. Of those that a mesh axis runs over, the one named last changes fastest.
Arguments:
- velocities: float32 [3, 5242880], P(None, ('gx', 'gy', 'gz')), may hold values from -6 to 6
- particle_cells: int32 [2, 5242880], P(None, ('gx', 'gy', 'gz')), may hold values from 0 to 4095
- grid_shift: int32 [2, 3], replicated, may hold values from -1 to 1, as said below
- axis_index: int32 [2, 16, 32, 1024], P(None, 'gx', 'gy', 'gz'), may hold values from 0 to 7
- migrate_dir: int32 [5242880], P(('gx', 'gy', 'gz')), may hold values from 0 to 6, as said below
- migrate_slot: int32 [5242880], P(('gx', 'gy', 'gz')), may hold values from 0 to 159, as said below
- contact_colloid: int32 [262144], P(('gx', 'gy', 'gz')), may hold values from 0 to 32767, as said below
- contact_particle: int32 [262144], P(('gx', 'gy', 'gz')), may hold values from 0 to 40959
- contact_weight: float32 [262144], P(('gx', 'gy', 'gz')), may hold values from 0.05 to 1
- colloid_velocity: float32 [3, 32768], P(None, ('gx', 'gy', 'gz')), may hold values from -6 to 6
Outputs:
- cell_velocity: float32 [3, 16, 32, 1024], P(None, 'gx', 'gy', 'gz')
- migrated: float32 [3, 5365760], P(None, ('gx', 'gy', 'gz'))
- colloid_force: float32 [3, 32768], P(None, ('gx', 'gy', 'gz'))
The draws below stay inside these ranges and needn't reach their ends.
Inputs may be any that keep to these rules, and one draw needn't show every extreme that they name: `grid_shift`: every entry is -1 or 1, and along every dimension the sign changes from each step to the next. `migrate_dir`: code 0 keeps a particle on its device. On every device at most 160 particles take any one nonzero code, and on every device some nonzero code is taken by exactly 160 particles. `migrate_slot`: among the particles of one device with the same nonzero code, the slots are distinct and run from 0 to that code's count minus 1; the slot is 0 where the code is 0. `contact_colloid`: the owner of every contact's colloid is the contact's own device or one of its six face neighbours along gx, gy, gz (periodic).
All inputs are finite; a program needn't handle non-finite values.
Results may differ from the reference program's by a relative error of at most 0.00015.
Values sent between devices are 32-bit elements; how exact they have to be, the bound alone decides.
No kernel may reach another device: no remote copies, remote signals or barrier semaphores. Data moves between devices by JAX's collectives and lax.ppermute only.
A program may use at most 128 MiB of HBM per device.

```python
import math
import jax
import jax.numpy as jnp
import numpy as np

CX = 4
CY = 8
CZ = 128
STEPS = 2
COLLOIDS_PER_UNIT = 256
P_DEV = 40960
CAP = 160
CONTACTS_PER_UNIT = 2048
NX = 16
NY = 32
NZ = 1024
PARTICLES = 5242880
COLLOIDS = 32768
CONTACTS = 262144
N_GX = 4
N_GY = 4
N_GZ = 8


def draw_grid_shift(key, part):
    signs = 2 * jax.random.randint(jax.random.fold_in(key, 3), (3,), 0, 2) - 1
    flips = jnp.where(jnp.arange(STEPS) % 2 == 0, 1, -1)
    return (flips[:, None] * signs[None, :]).astype(jnp.int32)


def migration_codes(key):
    base = jax.random.fold_in(key, 7)
    device_list = PARTICLES // P_DEV

    def device_codes(device):
        device_key = jax.random.fold_in(base, device)
        key_count, key_forced, key_order = jax.random.split(device_key, 3)
        counts = jax.random.randint(key_count, (6,), CAP // 4, CAP + 1)
        forced = jax.random.randint(key_forced, (), 0, 6)
        counts = jnp.where(jnp.arange(6) == forced, CAP, counts)
        ends = jnp.cumsum(counts)
        starts = ends - counts
        rank = jnp.arange(P_DEV)
        inside = rank < ends[5]
        number = jnp.sum((rank[:, None] >= ends[None, :]).astype(jnp.int32), axis=1)
        codes = jnp.where(inside, 1 + number, 0).astype(jnp.int32)
        places = jnp.where(inside, rank - starts[jnp.clip(number, 0, 5)], 0).astype(jnp.int32)
        order = jax.random.permutation(key_order, P_DEV)
        dirs = jnp.zeros((P_DEV,), jnp.int32).at[order].set(codes)
        slots = jnp.zeros((P_DEV,), jnp.int32).at[order].set(places)
        return (dirs, slots)
    dirs, slots = jax.vmap(device_codes)(jnp.arange(device_list))
    return (dirs.reshape(-1), slots.reshape(-1))


def draw_migrate_dir(key, part):
    return migration_codes(key)[0]


def draw_migrate_slot(key, part):
    return migration_codes(key)[1]


def draw_contact_colloid(key, part):
    grid_x = NX // CX
    grid_y = NY // CY
    grid_z = NZ // CZ
    device_list = grid_x * grid_y * grid_z
    key_near, member_key = jax.random.split(jax.random.fold_in(key, 11))
    neighbour = jax.random.randint(key_near, (device_list, CONTACTS_PER_UNIT), 0, 7)
    member_index = jax.random.randint(member_key, (device_list, CONTACTS_PER_UNIT), 0, COLLOIDS_PER_UNIT)
    moves = jnp.asarray(np.array([[0, 0, 0], [1, 0, 0], [-1, 0, 0], [0, 1, 0], [0, -1, 0], [0, 0, 1], [0, 0, -1]], dtype=np.int32))
    offsets = moves[neighbour]
    device = jnp.arange(device_list, dtype=jnp.int32)[:, None]
    place_x = device // (grid_y * grid_z)
    place_y = device // grid_z % grid_y
    place_z = device % grid_z
    owning_device = ((place_x + offsets[..., 0]) % grid_x * grid_y + (place_y + offsets[..., 1]) % grid_y) * grid_z + (place_z + offsets[..., 2]) % grid_z
    return (owning_device * COLLOIDS_PER_UNIT + member_index).reshape(-1).astype(jnp.int32)


def place_ends(values, own_key, least, high):
    dims = values.shape
    place = [jax.random.randint(jax.random.fold_in(own_key, axis), (), 0, dims[axis]) for axis in range(len(dims))]
    values = values.at[tuple(place)].set(least)
    longest = dims.index(max(dims))
    place[longest] = (place[longest] + 1) % dims[longest]
    return values.at[tuple(place)].set(high)


def block_levels(stream_key, dims, pieces, least, top_value):
    gain = 1.0
    for axis_at, parts in pieces:
        draws = jax.random.uniform(jax.random.fold_in(jax.random.fold_in(stream_key, 6), axis_at), (parts,), jnp.float32, least / len(pieces), top_value / len(pieces))
        gain = gain * jnp.repeat(jnp.exp(draws), dims[axis_at] // parts).reshape((-1,) + (1,) * (len(dims) - 1 - axis_at))
    return gain


def noise(rng, shape, deviation, limit, shards=(), kind=jnp.bfloat16):
    result = deviation * jax.random.normal(rng, shape, jnp.float32)
    if shards:
        result = result * block_levels(rng, shape, shards, -0.22, 0.18)
    return jnp.clip(result, -limit, limit).astype(kind)


def setup_inputs(seed: int = 0) -> dict:
    keys = jax.random.split(jax.random.key(seed), 11)
    velocities = noise(keys[0], (3, PARTICLES), 1.0, 6.0, ((1, 128),), jnp.float32)
    particle_cells = place_ends(jax.random.randint(keys[1], (STEPS, PARTICLES), 0, CX * CY * CZ), jax.random.fold_in(keys[1], 1), 0, (CX * CY * CZ) - 1).astype(jnp.int32)
    grid_shift = draw_grid_shift(jax.random.fold_in(keys[10], 71), 0)
    axis_index = place_ends(jax.random.randint(keys[3], (STEPS, NX, NY, NZ), 0, 8), jax.random.fold_in(keys[3], 1), 0, 7).astype(jnp.int32)
    migrate_dir = draw_migrate_dir(jax.random.fold_in(keys[10], 71), 0)
    migrate_slot = draw_migrate_slot(jax.random.fold_in(keys[10], 71), 0)
    contact_colloid = draw_contact_colloid(jax.random.fold_in(keys[10], 71), 0)
    contact_particle = place_ends(jax.random.randint(keys[7], (CONTACTS,), 0, P_DEV), jax.random.fold_in(keys[7], 1), 0, P_DEV - 1).astype(jnp.int32)
    contact_weight = jnp.clip(jnp.exp(math.log(1.0) - 2.9957323 * jax.random.uniform(keys[8], (CONTACTS,), jnp.float32) ** block_levels(keys[8], (CONTACTS,), ((0, 128),), -0.2, 0.2)), 0.05, 1.0)
    colloid_velocity = noise(keys[9], (3, COLLOIDS), 1.0, 6.0, ((1, 128),), jnp.float32)
    return dict(velocities=velocities, particle_cells=particle_cells, grid_shift=grid_shift, axis_index=axis_index, migrate_dir=migrate_dir, migrate_slot=migrate_slot, contact_colloid=contact_colloid, contact_particle=contact_particle, contact_weight=contact_weight, colloid_velocity=colloid_velocity)


def rotation_table():
    angle = 130.0 * math.pi / 180.0
    cosine = math.cos(angle)
    sine_value = math.sin(angle)
    entries = []
    for number in range(8):
        signs = [1.0 if number >> bit & 1 else -1.0 for bit in range(3)]
        unit = np.array(signs) / math.sqrt(3.0)
        cross = np.array([[0.0, -unit[2], unit[1]], [unit[2], 0.0, -unit[0]], [-unit[1], unit[0], 0.0]])
        matrix = cosine * np.eye(3) + (1.0 - cosine) * np.outer(unit, unit) + sine_value * cross
        entries.append(matrix.reshape(9))
    return np.array(entries)

def cell_rotation(axis_ids, table):
    matrix = jnp.zeros((9,) + axis_ids.shape, jnp.float32)
    for number in range(8):
        chosen = jnp.where(axis_ids == number, 1.0, 0.0).astype(jnp.float32)
        matrix = matrix + chosen[None] * table[number].reshape((9,) + (1,) * axis_ids.ndim)
    return matrix

def apply_rotation(matrix, vector):
    rows = [matrix[3 * row] * vector[0] + matrix[3 * row + 1] * vector[1] + matrix[3 * row + 2] * vector[2] for row in range(3)]
    return jnp.stack(rows)

def reference(velocities, particle_cells, grid_shift, axis_index, migrate_dir, migrate_slot, contact_colloid, contact_particle, contact_weight, colloid_velocity):
    table = jnp.asarray(rotation_table(), jnp.float32)
    cell_total = NX * NY * NZ
    device = (jnp.arange(PARTICLES) // P_DEV).astype(jnp.int32)
    device_x = device // (N_GY * N_GZ)
    device_y = device // N_GZ % N_GY
    device_z = device % N_GZ
    velocity_now = velocities
    mean = jnp.zeros((3, cell_total), jnp.float32)
    for step in range(STEPS):
        local = particle_cells[step]
        cell_x = (device_x * CX + local // (CY * CZ) + grid_shift[step, 0]) % NX
        cell_y = (device_y * CY + local // CZ % CY + grid_shift[step, 1]) % NY
        cell_z = (device_z * CZ + local % CZ + grid_shift[step, 2]) % NZ
        cell = ((cell_x * NY + cell_y) * NZ + cell_z).astype(jnp.int32)
        momentum = jnp.zeros((3, cell_total), jnp.float32).at[:, cell].add(velocity_now)
        counts = jnp.zeros((cell_total,), jnp.float32).at[cell].add(1.0)
        mean = momentum / jnp.maximum(counts, 1.0)
        matrix = cell_rotation(axis_index[step].reshape(-1), table)
        offset = mean - apply_rotation(matrix, mean)
        velocity_now = apply_rotation(matrix[:, cell], velocity_now) + offset[:, cell]
    cell_velocity = mean.reshape(3, NX, NY, NZ)
    device_list = PARTICLES // P_DEV
    leaving = migrate_dir > 0
    target = jnp.where(leaving, device * (6 * CAP) + (migrate_dir - 1) * CAP + migrate_slot, device_list * 6 * CAP).astype(jnp.int32)
    outbox = jnp.zeros((3, device_list * 6 * CAP), jnp.float32).at[:, target].set(velocity_now, mode='drop')
    outbox = outbox.reshape(3, N_GX, N_GY, N_GZ, 6, CAP)
    moves = ((1, 1), (1, -1), (2, 1), (2, -1), (3, 1), (3, -1))
    arrivals = [jnp.roll(outbox[:, :, :, :, number, :], sign, axis=dim) for number, (dim, sign) in enumerate(moves)]
    arrivals = jnp.stack(arrivals, axis=4).reshape(3, device_list, 6 * CAP)
    kept = jnp.where(leaving[None], 0.0, velocity_now).reshape(3, device_list, P_DEV)
    migrated = jnp.concatenate([kept, arrivals], axis=2).reshape(3, device_list * (P_DEV + 6 * CAP))
    contact_device = (jnp.arange(CONTACTS) // CONTACTS_PER_UNIT).astype(jnp.int32)
    particle = (contact_device * P_DEV + contact_particle).astype(jnp.int32)
    weighted = contact_weight[None] * velocity_now[:, particle]
    sum_wv = jnp.zeros((3, COLLOIDS), jnp.float32).at[:, contact_colloid].add(weighted)
    sum_w = jnp.zeros((COLLOIDS,), jnp.float32).at[contact_colloid].add(contact_weight)
    colloid_force = (sum_wv - sum_w * colloid_velocity) / jnp.maximum(sum_w, 1.0)
    return (cell_velocity, migrated, colloid_force)
```

```python
import math

import jax
import jax.numpy as jnp
from jax import lax
from jax.experimental import pallas as pl
from jax.experimental.pallas import tpu as pltpu
from jax.sharding import PartitionSpec as P

COLLOIDS_PER_UNIT = 256
CAP = 160
LANES = 128
BLOCK = 2048
SUB = 1024
CONTACT_BLOCK = 512
ANGLE = 130.0 * math.pi / 180.0
COS = math.cos(ANGLE)
ALONG = (1.0 - math.cos(ANGLE)) / 3.0
ACROSS = math.sin(ANGLE) / math.sqrt(3.0)
VMEM_LIMIT = 48 << 20


def split(x):
    high = x.astype(jnp.bfloat16).astype(jnp.float32)
    return high, x - high


def one_hot(ids, rows):
    places = lax.broadcasted_iota(jnp.int32, (rows, ids.shape[1]), 0)
    return jnp.where(places == ids, 1.0, 0.0).astype(jnp.bfloat16)


def row_mask(ids, rows):
    return lax.broadcasted_iota(jnp.int32, (rows, ids.shape[1]), 0) == ids


def spread(mask, values):
    return jnp.concatenate([jnp.where(mask, v, 0.0).astype(jnp.bfloat16) for v in values], axis=0)


def add_up(left, right):
    return lax.dot_general(
        left, right, (((1,), (1,)), ((), ())), preferred_element_type=jnp.float32
    )


def rotate(axis, v):
    e = [jnp.where((axis >> bit & 1) == 1, 1.0, -1.0) for bit in range(3)]
    d = (e[0] * v[0] + e[1] * v[1] + e[2] * v[2]) * ALONG
    return [
        COS * v[i]
        + e[i] * d
        + ACROSS * (e[(i + 1) % 3] * v[(i + 2) % 3] - e[(i + 2) % 3] * v[(i + 1) % 3])
        for i in range(3)
    ]


def cell_sums(v, cells):
    mask = row_mask(cells >> 7, 32)
    parts = [split(row) for row in v]
    ones = jnp.ones_like(v[0])
    left = spread(mask, [p[0] for p in parts] + [p[1] for p in parts] + [ones])
    return add_up(left, one_hot(cells & 127, LANES))


def mean_of(total):
    return (total[0:96] + total[96:192]) / jnp.maximum(
        jnp.concatenate([total[192:224]] * 3, axis=0), 1.0
    )


def cell_table(mean, axis):
    m = [mean[32 * i : 32 * i + 32] for i in range(3)]
    turned = rotate(axis, m)
    offset = jnp.concatenate([m[i] - turned[i] for i in range(3)], axis=0)
    high, low = split(offset)
    high = jnp.concatenate([high, axis.astype(jnp.float32)], axis=0)
    low = jnp.concatenate([low, jnp.zeros_like(m[0])], axis=0)
    return jnp.concatenate([high, low], axis=1).astype(jnp.bfloat16)


def pick(table, ids, rows):
    hot = one_hot(ids & 127, LANES)
    wide = jnp.dot(
        table, jnp.concatenate([hot, hot], axis=0), preferred_element_type=jnp.float32
    )
    mask = row_mask(ids >> 7, rows)
    return [
        jnp.sum(jnp.where(mask, wide[rows * f : rows * f + rows], 0.0), axis=0, keepdims=True)
        for f in range(wide.shape[0] // rows)
    ]


def collide(table, cells, v):
    picked = pick(table, cells, 32)
    turned = rotate(picked[3].astype(jnp.int32), v)
    return [turned[i] + picked[i] for i in range(3)]


def blocks_of(count):
    return count // BLOCK


def sum_kernel(v_ref, cells_ref, mean_ref, total):
    total[...] = jnp.zeros_like(total)

    def step(i, carry):
        for part in range(BLOCK // SUB):
            at = pl.ds(pl.multiple_of(i * BLOCK + part * SUB, SUB), SUB)
            v = [v_ref[c : c + 1, at] for c in range(3)]
            total[...] += cell_sums(v, cells_ref[0:1, at])
        return carry

    lax.fori_loop(0, blocks_of(v_ref.shape[1]), step, 0)
    mean_ref[...] = mean_of(total[...])


def turn_kernel(v_ref, cells_ref, mean_ref, axis_ref, out_ref, next_ref, total, table):
    total[...] = jnp.zeros_like(total)
    table[...] = cell_table(mean_ref[...], axis_ref[...])

    def step(i, carry):
        for part in range(BLOCK // SUB):
            at = pl.ds(pl.multiple_of(i * BLOCK + part * SUB, SUB), SUB)
            v = [v_ref[c : c + 1, at] for c in range(3)]
            new = collide(table[...], cells_ref[0:1, at], v)
            for c in range(3):
                out_ref[c : c + 1, at] = new[c]
            total[...] += cell_sums(new, cells_ref[1:2, at])
        return carry

    lax.fori_loop(0, blocks_of(v_ref.shape[1]), step, 0)
    next_ref[...] = mean_of(total[...])


def last_kernel(
    v_ref,
    cells_ref,
    mean_ref,
    axis_ref,
    dir_ref,
    slot_ref,
    particle_ref,
    place_ref,
    weight_ref,
    kept_ref,
    moved_ref,
    force_ref,
    moved,
    table,
    held,
):
    moved[...] = jnp.zeros_like(moved)
    table[...] = cell_table(mean_ref[...], axis_ref[...])
    rows = SUB // LANES

    def step(i, carry):
        for part in range(BLOCK // SUB):
            start = pl.multiple_of(i * BLOCK + part * SUB, SUB)
            at = pl.ds(start, SUB)
            v = [v_ref[c : c + 1, at] for c in range(3)]
            new = collide(table[...], cells_ref[1:2, at], v)
            code = dir_ref[0:1, at]
            key = jnp.where(code > 0, (code - 1) * 256 + slot_ref[0:1, at], 4096)
            line = pl.multiple_of(i * (BLOCK // LANES) + part * rows, rows)
            for c in range(3):
                kept_ref[c : c + 1, at] = jnp.where(code > 0, 0.0, new[c])
                held[c, pl.ds(line, rows), :] = new[c].reshape(rows, LANES)
            parts = [split(row) for row in new]
            left = spread(row_mask(key >> 7, 16), [p[0] for p in parts] + [p[1] for p in parts])
            moved[...] += add_up(left, one_hot(key & 127, LANES))
        return carry

    lax.fori_loop(0, blocks_of(v_ref.shape[1]), step, 0)
    moved_ref[...] = moved[0:48] + moved[48:96]

    lines = held.shape[1]
    high, low = split(held[...].reshape(3 * lines, LANES))
    wide = jnp.concatenate([high, low], axis=1).astype(jnp.bfloat16)
    force = jnp.zeros((128, LANES), jnp.float32)
    for part in range(particle_ref.shape[1] // CONTACT_BLOCK):
        at = slice(part * CONTACT_BLOCK, (part + 1) * CONTACT_BLOCK)
        weight = weight_ref[0:1, at]
        terms = [weight * row for row in pick(wide, particle_ref[0:1, at], lines)] + [weight]
        place = place_ref[0:1, at]
        parts = [split(row) for row in terms]
        left = spread(row_mask(place >> 7, 16), [p[0] for p in parts] + [p[1] for p in parts])
        force = force + add_up(left, one_hot(place & 127, LANES))
    force_ref[...] = force[0:64] + force[64:128]


def call(kernel, name, outs, scratch, flops, args):
    vmem = pl.BlockSpec(memory_space=pltpu.VMEM)
    return pl.pallas_call(
        kernel,
        name=name,
        out_shape=[jax.ShapeDtypeStruct(shape, jnp.float32) for shape in outs],
        in_specs=[vmem] * len(args),
        out_specs=[vmem] * len(outs),
        scratch_shapes=scratch,
        compiler_params=pltpu.CompilerParams(vmem_limit_bytes=VMEM_LIMIT),
        cost_estimate=pl.CostEstimate(flops=flops, bytes_accessed=2 << 20, transcendentals=0),
    )(*args)


def ring(axis, by):
    count = lax.axis_size(axis)
    return [(i, (i + by) % count) for i in range(count)]


def first(x, dim):
    return lax.slice_in_dim(x, 0, 1, axis=dim)


def last(x, dim):
    return lax.slice_in_dim(x, x.shape[dim] - 1, x.shape[dim], axis=dim)


def ahead(x, rim, dim):
    return jnp.concatenate([lax.slice_in_dim(x, 1, x.shape[dim], axis=dim), rim], axis=dim)


def behind(x, rim, dim):
    return jnp.concatenate([rim, lax.slice_in_dim(x, 0, x.shape[dim] - 1, axis=dim)], axis=dim)


def shifted_axes(axis_index, up):
    at = axis_index
    for dim, axis in enumerate(("gx", "gy", "gz")):
        rise = jnp.where(up[dim], at[0], at[1])
        fall = jnp.where(up[dim], at[1], at[0])
        upper = lax.ppermute(first(rise, dim), axis, ring(axis, -1))
        lower = lax.ppermute(last(fall, dim), axis, ring(axis, 1))
        rise = ahead(rise, upper, dim)
        fall = behind(fall, lower, dim)
        at = jnp.stack([jnp.where(up[dim], rise, fall), jnp.where(up[dim], fall, rise)])
    return at


def body(
    velocities,
    particle_cells,
    grid_shift,
    axis_index,
    migrate_dir,
    migrate_slot,
    contact_colloid,
    contact_particle,
    contact_weight,
    colloid_velocity,
):
    particles = velocities.shape[1]
    contacts = contact_colloid.shape[0]
    cells_x, cells_y, cells_z = axis_index.shape[1:]
    up = [grid_shift[0, dim] > 0 for dim in range(3)]

    size_x = lax.axis_size("gx")
    size_y = lax.axis_size("gy")
    size_z = lax.axis_size("gz")
    owner = contact_colloid // COLLOIDS_PER_UNIT
    apart_x = (owner // (size_y * size_z) - lax.axis_index("gx")) % size_x
    apart_y = (owner // size_z % size_y - lax.axis_index("gy")) % size_y
    apart_z = (owner % size_z - lax.axis_index("gz")) % size_z
    code = jnp.where(apart_z == 1, 5, jnp.where(apart_z == size_z - 1, 6, 0))
    code = jnp.where(apart_y == 1, 3, jnp.where(apart_y == size_y - 1, 4, code))
    code = jnp.where(apart_x == 1, 1, jnp.where(apart_x == size_x - 1, 2, code))
    place = code * COLLOIDS_PER_UNIT + contact_colloid % COLLOIDS_PER_UNIT

    axes = shifted_axes(axis_index, up).reshape(2, cells_x * cells_y, cells_z)
    total = pltpu.VMEM((224, LANES), jnp.float32)
    table = pltpu.VMEM((128, 256), jnp.bfloat16)
    pair_flops = 2 * 224 * 128 * particles
    (mean0,) = call(
        sum_kernel, "sums", [(96, LANES)], [total], pair_flops, (velocities, particle_cells)
    )
    moving, mean1 = call(
        turn_kernel,
        "turn",
        [(3, particles), (96, LANES)],
        [total, table],
        2 * pair_flops,
        (velocities, particle_cells, mean0, axes[0]),
    )
    kept, moved, force = call(
        last_kernel,
        "last",
        [(3, particles + 6 * CAP), (48, LANES), (64, LANES)],
        [
            pltpu.VMEM((96, LANES), jnp.float32),
            table,
            pltpu.VMEM((3, particles // LANES, LANES), jnp.float32),
        ],
        2 * pair_flops,
        (
            moving,
            particle_cells,
            mean1,
            axes[1],
            migrate_dir.reshape(1, particles),
            migrate_slot.reshape(1, particles),
            contact_particle.reshape(1, contacts),
            place.reshape(1, contacts),
            contact_weight.reshape(1, contacts),
        ),
    )
    moved = moved.reshape(3, 16, LANES)
    force = force.reshape(4, 16, LANES)
    mean = mean1.reshape(3, cells_x, cells_y, cells_z)
    sums = force[:, 0:2].reshape(4, COLLOIDS_PER_UNIT)
    arrivals = []
    for dim, axis in enumerate(("gx", "gy", "gz")):
        rims = (last(mean, dim + 1), first(mean, dim + 1))
        got = []
        for side, by in enumerate((1, -1)):
            number = 2 * dim + side
            sent = jnp.concatenate(
                [
                    moved[:, 2 * number : 2 * number + 2].reshape(-1),
                    force[:, 2 * number + 2 : 2 * number + 4].reshape(-1),
                    rims[side].reshape(-1),
                ]
            )
            came = lax.ppermute(sent, axis, ring(axis, by))
            arrivals.append(came[0:768].reshape(3, 256)[:, :CAP])
            sums = sums + came[768:1792].reshape(4, COLLOIDS_PER_UNIT)
            got.append(came[1792:].reshape(rims[side].shape))
        mean = jnp.where(up[dim], ahead(mean, got[1], dim + 1), behind(mean, got[0], dim + 1))
    migrated = lax.dynamic_update_slice(kept, jnp.concatenate(arrivals, axis=1), (0, particles))
    colloid_force = (sums[0:3] - sums[3:4] * colloid_velocity) / jnp.maximum(sums[3:4], 1.0)
    return (mean, migrated, colloid_force)


def solution(mesh):
    flat = P(("gx", "gy", "gz"))
    tall = P(None, ("gx", "gy", "gz"))
    grid = P(None, "gx", "gy", "gz")
    return jax.shard_map(
        body,
        mesh=mesh,
        in_specs=(tall, tall, P(), grid, flat, flat, flat, flat, flat, tall),
        out_specs=(grid, tall, tall),
        check_vma=False,
    )
```

```python
import math

import jax
import jax.numpy as jnp
from jax import lax
from jax.experimental import pallas as pl
from jax.experimental.pallas import tpu as pltpu
from jax.sharding import PartitionSpec as P

COLLOIDS_PER_UNIT = 256
CAP = 160
LANES = 128
UNROLL = 4
ANGLE = 130.0 * math.pi / 180.0
COS = math.cos(ANGLE)
ALONG = (1.0 - math.cos(ANGLE)) / 3.0
ACROSS = math.sin(ANGLE) / math.sqrt(3.0)
VMEM_LIMIT = 48 << 20


def split(x):
    high = x.astype(jnp.bfloat16).astype(jnp.float32)
    return high, x - high


def places(rows):
    return lax.broadcasted_iota(jnp.int32, (rows, LANES), 0).astype(jnp.float32).astype(jnp.bfloat16)


def narrow(row, rows):
    part = jnp.broadcast_to(row, (16, LANES)).astype(jnp.bfloat16)
    return jnp.concatenate([part] * (rows // 16), axis=0)


def one_hot(row, lanes):
    one, zero = jnp.asarray(1, jnp.bfloat16), jnp.asarray(0, jnp.bfloat16)
    return jnp.where(lanes == narrow(row, LANES), one, zero)


def add_up(left, right):
    return lax.dot_general(
        left, right, (((1,), (1,)), ((), ())), preferred_element_type=jnp.float32
    )


def fold(parts):
    rows = lax.broadcasted_iota(jnp.int32, parts[0].shape, 0)
    step = len(parts) // 2
    while step:
        low = (rows & step) == 0
        parts = [
            jnp.where(low, p + pltpu.roll(p, 8 - step, 0), q + pltpu.roll(q, step, 0))
            for p, q in zip(parts[:step], parts[step:])
        ]
        step //= 2
    return parts[0]


def rotate(axis, v):
    e = [jnp.where((axis >> bit & 1) == 1, 1.0, -1.0) for bit in range(3)]
    d = (e[0] * v[0] + e[1] * v[1] + e[2] * v[2]) * ALONG
    return [
        COS * v[i]
        + e[i] * d
        + ACROSS * (e[(i + 1) % 3] * v[(i + 2) % 3] - e[(i + 2) % 3] * v[(i + 1) % 3])
        for i in range(3)
    ]


def scatter(values, ids, rows, counted, lanes):
    low = (ids & (LANES - 1)).astype(jnp.float32)
    line = (ids >> 7).astype(jnp.float32)
    parts = [split(x) for x in values]
    parts = [p[0] for p in parts] + [p[1] for p in parts]
    spots = places(rows)
    one, zero = jnp.asarray(1, jnp.bfloat16), jnp.asarray(0, jnp.bfloat16)
    left, right = [], []
    for j in range(8):
        mask = spots == narrow(line[j : j + 1], rows)
        lines = [jnp.where(mask, narrow(x[j : j + 1], rows), zero) for x in parts]
        if counted:
            lines.append(jnp.where(mask, one, zero))
        left.append(jnp.concatenate(lines, axis=0))
        right.append(one_hot(low[j : j + 1], lanes))
    return add_up(jnp.concatenate(left, axis=1), jnp.concatenate(right, axis=1))


def mean_of(total):
    return (total[0:96] + total[96:192]) / jnp.maximum(
        jnp.concatenate([total[192:224]] * 3, axis=0), 1.0
    )


def cell_table(mean, axis):
    m = [mean[32 * i : 32 * i + 32] for i in range(3)]
    turned = rotate(axis, m)
    offset = jnp.concatenate([m[i] - turned[i] for i in range(3)], axis=0)
    high, low = split(offset)
    high = jnp.concatenate([high, axis.astype(jnp.float32)], axis=0)
    low = jnp.concatenate([low, jnp.zeros_like(m[0])], axis=0)
    return jnp.concatenate([high, low], axis=1).astype(jnp.bfloat16)


def pick(table, ids, rows, lanes):
    low = (ids & (LANES - 1)).astype(jnp.float32)
    line = ids >> 7
    spots = lax.broadcasted_iota(jnp.int32, (rows, LANES), 0)
    count = table.shape[0] // rows
    parts = [[] for _ in range(count)]
    for j in range(0, 8, 2):
        hot = jnp.concatenate([one_hot(low[j + k : j + k + 1], lanes) for k in range(2)], axis=1)
        wide = jnp.dot(
            table, jnp.concatenate([hot, hot], axis=0), preferred_element_type=jnp.float32
        )
        for k in range(2):
            mask = spots == jnp.broadcast_to(line[j + k : j + k + 1], (rows, LANES))
            for f in range(count):
                found = wide[rows * f : rows * f + rows, k * LANES : (k + 1) * LANES]
                found = jnp.where(mask, found, 0.0)
                parts[f].append(jnp.sum(found.reshape(rows // 8, 8, LANES), axis=0))
    return [fold(p) for p in parts]


def collide(table, cells, v, lanes):
    picked = pick(table, cells, 32, lanes)
    turned = rotate(picked[3].astype(jnp.int32), v)
    return [turned[i] + picked[i] for i in range(3)]


def sum_kernel(v_ref, cells_ref, mean_ref, total):
    total[...] = jnp.zeros_like(total)

    def step(i, carry):
        lanes = places(LANES)
        added = 0.0
        for part in range(UNROLL):
            at = pl.ds(pl.multiple_of((i * UNROLL + part) * 8, 8), 8)
            v = [v_ref[at, c, :] for c in range(3)]
            added += scatter(v, cells_ref[at, 0, :], 32, True, lanes)
        total[...] += added
        return carry

    lax.fori_loop(0, v_ref.shape[0] // (8 * UNROLL), step, 0)
    mean_ref[...] = mean_of(total[...])


def turn_kernel(v_ref, cells_ref, mean_ref, axis_ref, out_ref, next_ref, total, table):
    total[...] = jnp.zeros_like(total)
    table[...] = cell_table(mean_ref[...], axis_ref[...])

    def step(i, carry):
        lanes = places(LANES)
        added = 0.0
        for part in range(UNROLL):
            at = pl.ds(pl.multiple_of((i * UNROLL + part) * 8, 8), 8)
            v = [v_ref[at, c, :] for c in range(3)]
            new = collide(table[...], cells_ref[at, 0, :], v, lanes)
            for c in range(3):
                out_ref[c, at, :] = new[c]
            added += scatter(new, cells_ref[at, 1, :], 32, True, lanes)
        total[...] += added
        return carry

    lax.fori_loop(0, v_ref.shape[0] // (8 * UNROLL), step, 0)
    next_ref[...] = mean_of(total[...])


def last_kernel(
    v_ref,
    cells_ref,
    mean_ref,
    axis_ref,
    dir_ref,
    slot_ref,
    particle_ref,
    place_ref,
    weight_ref,
    kept_ref,
    moved_ref,
    force_ref,
    moved,
    table,
    held,
):
    moved[...] = jnp.zeros_like(moved)
    table[...] = cell_table(mean_ref[...], axis_ref[...])

    def step(i, carry):
        lanes = places(LANES)
        added = 0.0
        for part in range(UNROLL):
            line = pl.multiple_of((i * UNROLL + part) * 8, 8)
            at = pl.ds(line, 8)
            v = [v_ref[c, at, :] for c in range(3)]
            new = collide(table[...], cells_ref[at, 1, :], v, lanes)
            code = dir_ref[at, :]
            for c in range(3):
                held[c, at, :] = new[c]
                kept = jnp.where(code > 0, 0.0, new[c])
                for j in range(8):
                    kept_ref[c : c + 1, pl.ds((line + j) * LANES, LANES)] = kept[j : j + 1]
            key = jnp.where(code > 0, (code - 1) * 256 + slot_ref[at, :], 4096)
            added += scatter(new, key, 16, False, lanes)
        moved[...] += added
        return carry

    lax.fori_loop(0, v_ref.shape[1] // (8 * UNROLL), step, 0)
    moved_ref[...] = moved[0:48] + moved[48:96]

    lines = held.shape[1]
    high, low = split(held[...].reshape(3 * lines, LANES))
    wide = jnp.concatenate([high, low], axis=1).astype(jnp.bfloat16)
    lanes = places(LANES)
    force = jnp.zeros((128, LANES), jnp.float32)
    for part in range(particle_ref.shape[0] // 8):
        at = slice(8 * part, 8 * part + 8)
        weight = weight_ref[at, :]
        terms = [weight * x for x in pick(wide, particle_ref[at, :], lines, lanes)] + [weight]
        force = force + scatter(terms, place_ref[at, :], 16, False, lanes)
    force_ref[...] = force[0:64] + force[64:128]


def call(kernel, name, outs, scratch, flops, args):
    vmem = pl.BlockSpec(memory_space=pltpu.VMEM)
    return pl.pallas_call(
        kernel,
        name=name,
        out_shape=[jax.ShapeDtypeStruct(shape, jnp.float32) for shape in outs],
        in_specs=[vmem] * len(args),
        out_specs=[vmem] * len(outs),
        scratch_shapes=scratch,
        compiler_params=pltpu.CompilerParams(vmem_limit_bytes=VMEM_LIMIT),
        cost_estimate=pl.CostEstimate(flops=flops, bytes_accessed=2 << 20, transcendentals=0),
    )(*args)


def ring(axis, by):
    count = lax.axis_size(axis)
    return [(i, (i + by) % count) for i in range(count)]


def first(x, dim):
    return lax.slice_in_dim(x, 0, 1, axis=dim)


def last(x, dim):
    return lax.slice_in_dim(x, x.shape[dim] - 1, x.shape[dim], axis=dim)


def ahead(x, rim, dim):
    return jnp.concatenate([lax.slice_in_dim(x, 1, x.shape[dim], axis=dim), rim], axis=dim)


def behind(x, rim, dim):
    return jnp.concatenate([rim, lax.slice_in_dim(x, 0, x.shape[dim] - 1, axis=dim)], axis=dim)


def shifted_axes(axis_index, up):
    at = axis_index
    for dim, axis in enumerate(("gx", "gy", "gz")):
        rise = jnp.where(up[dim], at[0], at[1])
        fall = jnp.where(up[dim], at[1], at[0])
        upper = lax.ppermute(first(rise, dim), axis, ring(axis, -1))
        lower = lax.ppermute(last(fall, dim), axis, ring(axis, 1))
        rise = ahead(rise, upper, dim)
        fall = behind(fall, lower, dim)
        at = jnp.stack([jnp.where(up[dim], rise, fall), jnp.where(up[dim], fall, rise)])
    return at


def body(
    velocities,
    particle_cells,
    grid_shift,
    axis_index,
    migrate_dir,
    migrate_slot,
    contact_colloid,
    contact_particle,
    contact_weight,
    colloid_velocity,
):
    particles = velocities.shape[1]
    cells_x, cells_y, cells_z = axis_index.shape[1:]
    up = [grid_shift[0, dim] > 0 for dim in range(3)]

    size_x = lax.axis_size("gx")
    size_y = lax.axis_size("gy")
    size_z = lax.axis_size("gz")
    owner = contact_colloid // COLLOIDS_PER_UNIT
    apart_x = (owner // (size_y * size_z) - lax.axis_index("gx")) % size_x
    apart_y = (owner // size_z % size_y - lax.axis_index("gy")) % size_y
    apart_z = (owner % size_z - lax.axis_index("gz")) % size_z
    code = jnp.where(apart_z == 1, 5, jnp.where(apart_z == size_z - 1, 6, 0))
    code = jnp.where(apart_y == 1, 3, jnp.where(apart_y == size_y - 1, 4, code))
    code = jnp.where(apart_x == 1, 1, jnp.where(apart_x == size_x - 1, 2, code))
    place = code * COLLOIDS_PER_UNIT + contact_colloid % COLLOIDS_PER_UNIT

    axes = shifted_axes(axis_index, up).reshape(2, cells_x * cells_y, cells_z)
    lines = particles // LANES
    velocity = velocities.reshape(3, lines, LANES).transpose(1, 0, 2)
    cells = particle_cells.reshape(2, lines, LANES).transpose(1, 0, 2)
    total = pltpu.VMEM((224, LANES), jnp.float32)
    table = pltpu.VMEM((128, 256), jnp.bfloat16)
    pair_flops = 2 * 224 * 128 * particles
    (mean0,) = call(
        sum_kernel, "sums", [(96, LANES)], [total], pair_flops, (velocity, cells)
    )
    moving, mean1 = call(
        turn_kernel,
        "turn",
        [(3, lines, LANES), (96, LANES)],
        [total, table],
        2 * pair_flops,
        (velocity, cells, mean0, axes[0]),
    )
    kept, moved, force = call(
        last_kernel,
        "last",
        [(3, particles + 6 * CAP), (48, LANES), (64, LANES)],
        [
            pltpu.VMEM((96, LANES), jnp.float32),
            table,
            pltpu.VMEM((3, lines, LANES), jnp.float32),
        ],
        2 * pair_flops,
        (
            moving,
            cells,
            mean1,
            axes[1],
            migrate_dir.reshape(lines, LANES),
            migrate_slot.reshape(lines, LANES),
            contact_particle.reshape(-1, LANES),
            place.reshape(-1, LANES),
            contact_weight.reshape(-1, LANES),
        ),
    )
    moved = moved.reshape(3, 16, LANES)
    force = force.reshape(4, 16, LANES)
    mean = mean1.reshape(3, cells_x, cells_y, cells_z)
    sums = force[:, 0:2].reshape(4, COLLOIDS_PER_UNIT)
    arrivals = []
    for dim, axis in enumerate(("gx", "gy", "gz")):
        rims = (last(mean, dim + 1), first(mean, dim + 1))
        got = []
        for side, by in enumerate((1, -1)):
            number = 2 * dim + side
            sent = jnp.concatenate(
                [
                    moved[:, 2 * number : 2 * number + 2].reshape(-1),
                    force[:, 2 * number + 2 : 2 * number + 4].reshape(-1),
                    rims[side].reshape(-1),
                ]
            )
            came = lax.ppermute(sent, axis, ring(axis, by))
            arrivals.append(came[0:768].reshape(3, 256)[:, :CAP])
            sums = sums + came[768:1792].reshape(4, COLLOIDS_PER_UNIT)
            got.append(came[1792:].reshape(rims[side].shape))
        mean = jnp.where(up[dim], ahead(mean, got[1], dim + 1), behind(mean, got[0], dim + 1))
    migrated = lax.dynamic_update_slice(kept, jnp.concatenate(arrivals, axis=1), (0, particles))
    colloid_force = (sums[0:3] - sums[3:4] * colloid_velocity) / jnp.maximum(sums[3:4], 1.0)
    return (mean, migrated, colloid_force)


def solution(mesh):
    flat = P(("gx", "gy", "gz"))
    tall = P(None, ("gx", "gy", "gz"))
    grid = P(None, "gx", "gy", "gz")
    return jax.shard_map(
        body,
        mesh=mesh,
        in_specs=(tall, tall, P(), grid, flat, flat, flat, flat, flat, tall),
        out_specs=(grid, tall, tall),
        check_vma=False,
    )
```

```python
import functools
import math

import jax
import jax.numpy as jnp
from jax import lax
from jax.experimental import pallas as pl
from jax.experimental.pallas import tpu as pltpu
from jax.sharding import PartitionSpec as P

COLLOIDS_PER_UNIT = 256
CAP = 160
LANES = 128
UNROLL = 4
ANGLE = 130.0 * math.pi / 180.0
COS = math.cos(ANGLE)
ALONG = (1.0 - math.cos(ANGLE)) / 3.0
ACROSS = math.sin(ANGLE) / math.sqrt(3.0)
VMEM_LIMIT = 48 << 20


def split(x):
    high = x.astype(jnp.bfloat16).astype(jnp.float32)
    return high, x - high


def places(rows):
    return lax.broadcasted_iota(jnp.int32, (rows, LANES), 0).astype(jnp.float32).astype(jnp.bfloat16)


def narrow(row, rows):
    part = jnp.broadcast_to(row, (16, LANES)).astype(jnp.bfloat16)
    return jnp.concatenate([part] * (rows // 16), axis=0)


def one_hot(row, lanes):
    one, zero = jnp.asarray(1, jnp.bfloat16), jnp.asarray(0, jnp.bfloat16)
    return jnp.where(lanes == narrow(row, LANES), one, zero)


def add_up(left, right):
    return lax.dot_general(
        left, right, (((1,), (1,)), ((), ())), preferred_element_type=jnp.float32
    )


def fold(parts):
    rows = lax.broadcasted_iota(jnp.int32, parts[0].shape, 0)
    step = len(parts) // 2
    while step:
        low = (rows & step) == 0
        parts = [
            jnp.where(low, p + pltpu.roll(p, 8 - step, 0), q + pltpu.roll(q, step, 0))
            for p, q in zip(parts[:step], parts[step:])
        ]
        step //= 2
    return parts[0]


def rotate(axis, v):
    e = [jnp.where((axis >> bit & 1) == 1, 1.0, -1.0) for bit in range(3)]
    d = (e[0] * v[0] + e[1] * v[1] + e[2] * v[2]) * ALONG
    return [
        COS * v[i]
        + e[i] * d
        + ACROSS * (e[(i + 1) % 3] * v[(i + 2) % 3] - e[(i + 2) % 3] * v[(i + 1) % 3])
        for i in range(3)
    ]


def scatter(values, ids, rows, counted, lanes):
    low = (ids & (LANES - 1)).astype(jnp.float32)
    line = (ids >> 7).astype(jnp.float32)
    parts = [split(x) for x in values]
    parts = [p[0] for p in parts] + [p[1] for p in parts]
    spots = places(rows)
    one, zero = jnp.asarray(1, jnp.bfloat16), jnp.asarray(0, jnp.bfloat16)
    left, right = [], []
    for j in range(8):
        mask = spots == narrow(line[j : j + 1], rows)
        lines = [jnp.where(mask, narrow(x[j : j + 1], rows), zero) for x in parts]
        if counted:
            lines.append(jnp.where(mask, one, zero))
        left.append(jnp.concatenate(lines, axis=0))
        right.append(one_hot(low[j : j + 1], lanes))
    return add_up(jnp.concatenate(left, axis=1), jnp.concatenate(right, axis=1))


def mean_of(total):
    return (total[0:96] + total[96:192]) / jnp.maximum(
        jnp.concatenate([total[192:224]] * 3, axis=0), 1.0
    )


def cell_table(mean, axis):
    m = [mean[32 * i : 32 * i + 32] for i in range(3)]
    turned = rotate(axis, m)
    offset = jnp.concatenate([m[i] - turned[i] for i in range(3)], axis=0)
    high, low = split(offset)
    high = jnp.concatenate([high, axis.astype(jnp.float32)], axis=0)
    low = jnp.concatenate([low, jnp.zeros_like(m[0])], axis=0)
    return jnp.concatenate([high, low], axis=1).astype(jnp.bfloat16)


def pick(table, ids, rows, lanes):
    low = (ids & (LANES - 1)).astype(jnp.float32)
    line = ids >> 7
    spots = lax.broadcasted_iota(jnp.int32, (rows, LANES), 0)
    count = table.shape[0] // rows
    parts = [[] for _ in range(count)]
    for j in range(0, 8, 2):
        hot = jnp.concatenate([one_hot(low[j + k : j + k + 1], lanes) for k in range(2)], axis=1)
        wide = jnp.dot(
            table, jnp.concatenate([hot, hot], axis=0), preferred_element_type=jnp.float32
        )
        for k in range(2):
            mask = spots == jnp.broadcast_to(line[j + k : j + k + 1], (rows, LANES))
            for f in range(count):
                found = wide[rows * f : rows * f + rows, k * LANES : (k + 1) * LANES]
                found = jnp.where(mask, found, 0.0)
                parts[f].append(jnp.sum(found.reshape(rows // 8, 8, LANES), axis=0))
    return [fold(p) for p in parts]


def collide(table, cells, v, lanes):
    picked = pick(table, cells, 32, lanes)
    turned = rotate(picked[3].astype(jnp.int32), v)
    return [turned[i] + picked[i] for i in range(3)]


def sum_kernel(low, high, ends, v_ref, cells_ref, *refs):
    done_ref, out_ref = (None, refs[-1]) if low == 0 else (refs[0], refs[-1])
    shape = (224, LANES)

    def step(i, total):
        lanes = places(LANES)
        for part in range(UNROLL):
            at = pl.ds(pl.multiple_of((i * UNROLL + part) * 8, 8), 8)
            v = [v_ref[at, c, :] for c in range(3)]
            total += scatter(v, cells_ref[at, 0, :], 32, True, lanes)
        return total

    total = jnp.zeros(shape, jnp.float32) if done_ref is None else done_ref[...]
    total = lax.fori_loop(low, high, step, total)
    out_ref[...] = mean_of(total) if ends else total


def turn_kernel(v_ref, cells_ref, mean_ref, axis_ref, out_ref, next_ref, total, table):
    total[...] = jnp.zeros_like(total)
    table[...] = cell_table(mean_ref[...], axis_ref[...])

    def step(i, carry):
        lanes = places(LANES)
        added = 0.0
        for part in range(UNROLL):
            at = pl.ds(pl.multiple_of((i * UNROLL + part) * 8, 8), 8)
            v = [v_ref[at, c, :] for c in range(3)]
            new = collide(table[...], cells_ref[at, 0, :], v, lanes)
            for c in range(3):
                out_ref[c, at, :] = new[c]
            added += scatter(new, cells_ref[at, 1, :], 32, True, lanes)
        total[...] += added
        return carry

    lax.fori_loop(0, v_ref.shape[0] // (8 * UNROLL), step, 0)
    next_ref[...] = mean_of(total[...])


def leave(low, high, v_ref, cells_ref, mean_ref, axis_ref, dir_ref, slot_ref, new_ref, first, moved, table):
    table[...] = cell_table(mean_ref[...], axis_ref[...])

    def step(i, carry):
        lanes = places(LANES)
        added = 0.0
        for part in range(UNROLL):
            line = pl.multiple_of((i * UNROLL + part) * 8, 8)
            at = pl.ds(line, 8)
            v = [v_ref[c, at, :] for c in range(3)]
            new = collide(table[...], cells_ref[at, 1, :], v, lanes)
            to = pl.ds(pl.multiple_of(line - first, 8), 8)
            for c in range(3):
                new_ref[c, to, :] = new[c]
            code = dir_ref[at, :]
            key = jnp.where(code > 0, (code - 1) * 256 + slot_ref[at, :], 4096)
            added += scatter(new, key, 16, False, lanes)
        moved[...] += added
        return carry

    lax.fori_loop(low, high, step, 0)


def part_kernel(low, high, *refs):
    inputs, refs = refs[:6], refs[6:]
    new_ref, moved_ref, table = refs[-3:]
    moved_ref[...] = jnp.zeros_like(moved_ref) if low == 0 else refs[0][...]
    leave(low, high, *inputs, new_ref, low * 8 * UNROLL, moved_ref, table)


def last_kernel(low, high, *refs):
    inputs, refs = refs[:6], refs[6:]
    before_ref, parts, refs = refs[0], refs[1:3], refs[3:]
    particle_ref, place_ref, weight_ref = refs[:3]
    kept_ref, moved_ref, force_ref, moved, table, held = refs[-6:]
    dir_ref = inputs[4]
    moved[...] = before_ref[...]
    start = 0
    for part in parts:
        held[:, start : start + part.shape[1], :] = part[...]
        start += part.shape[1]
    leave(low, high, *inputs, held, 0, moved, table)
    moved_ref[...] = moved[0:48] + moved[48:96]

    def keep(i, carry):
        line = pl.multiple_of(i * 8, 8)
        at = pl.ds(line, 8)
        stays = dir_ref[at, :] == 0
        for c in range(3):
            kept = jnp.where(stays, held[c, at, :], 0.0)
            for j in range(8):
                kept_ref[c : c + 1, pl.ds((line + j) * LANES, LANES)] = kept[j : j + 1]
        return carry

    lines = held.shape[1]
    lax.fori_loop(0, lines // 8, keep, 0, unroll=4)
    high_part, low_part = split(held[...].reshape(3 * lines, LANES))
    wide = jnp.concatenate([high_part, low_part], axis=1).astype(jnp.bfloat16)
    lanes = places(LANES)
    force = jnp.zeros((128, LANES), jnp.float32)
    for part in range(particle_ref.shape[0] // 8):
        at = slice(8 * part, 8 * part + 8)
        weight = weight_ref[at, :]
        terms = [weight * x for x in pick(wide, particle_ref[at, :], lines, lanes)] + [weight]
        force = force + scatter(terms, place_ref[at, :], 16, False, lanes)
    force_ref[...] = force[0:64] + force[64:128]


def call(kernel, name, outs, scratch, flops, args):
    vmem = pl.BlockSpec(memory_space=pltpu.VMEM)
    return pl.pallas_call(
        kernel,
        name=name,
        out_shape=[jax.ShapeDtypeStruct(shape, jnp.float32) for shape in outs],
        in_specs=[vmem] * len(args),
        out_specs=[vmem] * len(outs),
        scratch_shapes=scratch,
        compiler_params=pltpu.CompilerParams(vmem_limit_bytes=VMEM_LIMIT),
        cost_estimate=pl.CostEstimate(flops=flops, bytes_accessed=2 << 20, transcendentals=0),
    )(*args)


def ring(axis, by):
    count = lax.axis_size(axis)
    return [(i, (i + by) % count) for i in range(count)]


def first(x, dim):
    return lax.slice_in_dim(x, 0, 1, axis=dim)


def last(x, dim):
    return lax.slice_in_dim(x, x.shape[dim] - 1, x.shape[dim], axis=dim)


def ahead(x, rim, dim):
    return jnp.concatenate([lax.slice_in_dim(x, 1, x.shape[dim], axis=dim), rim], axis=dim)


def behind(x, rim, dim):
    return jnp.concatenate([rim, lax.slice_in_dim(x, 0, x.shape[dim] - 1, axis=dim)], axis=dim)


def axis_round(at, up, dim, axis):
    rise = jnp.where(up, at[0], at[1])
    fall = jnp.where(up, at[1], at[0])
    upper = lax.ppermute(first(rise, dim), axis, ring(axis, -1))
    lower = lax.ppermute(last(fall, dim), axis, ring(axis, 1))
    rise = ahead(rise, upper, dim)
    fall = behind(fall, lower, dim)
    at = jnp.stack([jnp.where(up, rise, fall), jnp.where(up, fall, rise)])
    return at, (upper, lower)


def mean_round(mean, up, dim, axis):
    lower = lax.ppermute(last(mean, dim + 1), axis, ring(axis, 1))
    upper = lax.ppermute(first(mean, dim + 1), axis, ring(axis, -1))
    mean = jnp.where(up, ahead(mean, upper, dim + 1), behind(mean, lower, dim + 1))
    return mean, (upper, lower)


def body(
    velocities,
    particle_cells,
    grid_shift,
    axis_index,
    migrate_dir,
    migrate_slot,
    contact_colloid,
    contact_particle,
    contact_weight,
    colloid_velocity,
):
    particles = velocities.shape[1]
    cells_x, cells_y, cells_z = axis_index.shape[1:]
    up = [grid_shift[0, dim] > 0 for dim in range(3)]

    size_x = lax.axis_size("gx")
    size_y = lax.axis_size("gy")
    size_z = lax.axis_size("gz")
    owner = contact_colloid // COLLOIDS_PER_UNIT
    apart_x = (owner // (size_y * size_z) - lax.axis_index("gx")) % size_x
    apart_y = (owner // size_z % size_y - lax.axis_index("gy")) % size_y
    apart_z = (owner % size_z - lax.axis_index("gz")) % size_z
    code = jnp.where(apart_z == 1, 5, jnp.where(apart_z == size_z - 1, 6, 0))
    code = jnp.where(apart_y == 1, 3, jnp.where(apart_y == size_y - 1, 4, code))
    code = jnp.where(apart_x == 1, 1, jnp.where(apart_x == size_x - 1, 2, code))
    place = code * COLLOIDS_PER_UNIT + contact_colloid % COLLOIDS_PER_UNIT

    lines = particles // LANES
    steps = lines // (8 * UNROLL)
    cuts = (0, steps * 3 // 10, steps * 6 // 10, steps)
    spans = tuple(zip(cuts[:-1], cuts[1:]))
    velocity = velocities.reshape(3, lines, LANES).transpose(1, 0, 2)
    cells = particle_cells.reshape(2, lines, LANES).transpose(1, 0, 2)
    total = pltpu.VMEM((224, LANES), jnp.float32)
    table = pltpu.VMEM((128, 256), jnp.bfloat16)
    pair_flops = 2 * 224 * 128 * particles

    axes = axis_index
    summed = ()
    for dim, axis in enumerate(("gx", "gy", "gz")):
        axes, rims = axis_round(axes, up[dim], dim, axis)
        low, high = spans[dim]
        ends = dim == 2
        (result,) = call(
            functools.partial(sum_kernel, low, high, ends),
            "sums_%d" % dim,
            [(96 if ends else 224, LANES)],
            [],
            pair_flops // 3,
            (velocity, cells) + summed,
        )
        summed = (result,) + rims
    mean0 = result
    axes = axes.reshape(2, cells_x * cells_y, cells_z)
    moving, mean1 = call(
        turn_kernel,
        "turn",
        [(3, lines, LANES), (96, LANES)],
        [total, table],
        2 * pair_flops,
        (velocity, cells, mean0, axes[0]),
    )
    shared = (
        moving,
        cells,
        mean1,
        axes[1],
        migrate_dir.reshape(lines, LANES),
        migrate_slot.reshape(lines, LANES),
    )
    mean = mean1.reshape(3, cells_x, cells_y, cells_z)
    tied = ()
    parts = []
    for dim, axis in enumerate(("gx", "gy")):
        mean, rims = mean_round(mean, up[dim], dim, axis)
        low, high = spans[dim]
        part, moved = call(
            functools.partial(part_kernel, low, high),
            "part_%d" % dim,
            [(3, (high - low) * 8 * UNROLL, LANES), (96, LANES)],
            [table],
            pair_flops // 2,
            shared + tied,
        )
        parts.append(part)
        tied = (moved,) + rims
    low, high = spans[2]
    kept, moved, force = call(
        functools.partial(last_kernel, low, high),
        "last",
        [(3, particles + 6 * CAP), (48, LANES), (64, LANES)],
        [
            pltpu.VMEM((96, LANES), jnp.float32),
            table,
            pltpu.VMEM((3, lines, LANES), jnp.float32),
        ],
        pair_flops,
        shared
        + (moved, *parts)
        + (
            contact_particle.reshape(-1, LANES),
            place.reshape(-1, LANES),
            contact_weight.reshape(-1, LANES),
        )
        + rims,
    )
    moved = moved.reshape(3, 16, LANES)
    force = force.reshape(4, 16, LANES)
    sums = force[:, 0:2].reshape(4, COLLOIDS_PER_UNIT)
    arrivals = []
    faces = (last(mean, 3), first(mean, 3))
    got = []
    for number in range(6):
        axis, by = ("gx", "gy", "gz")[number // 2], 1 - 2 * (number % 2)
        sent = [
            moved[:, 2 * number : 2 * number + 2].reshape(-1),
            force[:, 2 * number + 2 : 2 * number + 4].reshape(-1),
        ]
        if axis == "gz":
            sent.append(faces[number % 2].reshape(-1))
        came = lax.ppermute(jnp.concatenate(sent), axis, ring(axis, by))
        arrivals.append(came[0:768].reshape(3, 256)[:, :CAP])
        sums = sums + came[768:1792].reshape(4, COLLOIDS_PER_UNIT)
        if axis == "gz":
            got.append(came[1792:].reshape(faces[0].shape))
    mean = jnp.where(up[2], ahead(mean, got[1], 3), behind(mean, got[0], 3))
    migrated = lax.dynamic_update_slice(kept, jnp.concatenate(arrivals, axis=1), (0, particles))
    colloid_force = (sums[0:3] - sums[3:4] * colloid_velocity) / jnp.maximum(sums[3:4], 1.0)
    return (mean, migrated, colloid_force)


def solution(mesh):
    flat = P(("gx", "gy", "gz"))
    tall = P(None, ("gx", "gy", "gz"))
    grid = P(None, "gx", "gy", "gz")
    return jax.shard_map(
        body,
        mesh=mesh,
        in_specs=(tall, tall, P(), grid, flat, flat, flat, flat, flat, tall),
        out_specs=(grid, tall, tall),
        check_vma=False,
    )
```

```python
import functools
import math

import jax
import jax.numpy as jnp
from jax import lax
from jax.experimental import pallas as pl
from jax.experimental.pallas import tpu as pltpu
from jax.sharding import PartitionSpec as P

COLLOIDS_PER_UNIT = 256
CAP = 160
LANES = 128
UNROLL = 4
ANGLE = 130.0 * math.pi / 180.0
COS = math.cos(ANGLE)
ALONG = (1.0 - math.cos(ANGLE)) / 3.0
ACROSS = math.sin(ANGLE) / math.sqrt(3.0)
VMEM_LIMIT = 48 << 20


def split(x):
    high = x.astype(jnp.bfloat16).astype(jnp.float32)
    return high, x - high


def places(rows):
    return lax.broadcasted_iota(jnp.int32, (rows, LANES), 0).astype(jnp.float32).astype(jnp.bfloat16)


def narrow(row, rows):
    part = jnp.broadcast_to(row, (16, LANES)).astype(jnp.bfloat16)
    return jnp.concatenate([part] * (rows // 16), axis=0)


def one_hot(row, lanes):
    one, zero = jnp.asarray(1, jnp.bfloat16), jnp.asarray(0, jnp.bfloat16)
    return jnp.where(lanes == narrow(row, LANES), one, zero)


def add_up(left, right):
    return lax.dot_general(
        left, right, (((1,), (1,)), ((), ())), preferred_element_type=jnp.float32
    )


def fold(parts):
    rows = lax.broadcasted_iota(jnp.int32, parts[0].shape, 0)
    step = 1
    while len(parts) > 1:
        low = (rows & step) == 0
        parts = [
            jnp.where(low, p, q) + pltpu.roll(jnp.where(low, q, p), step, 0)
            for p, q in zip(parts[0::2], parts[1::2])
        ]
        step *= 2
    return parts[0]


def rotate(axis, v):
    e = [jnp.where((axis >> bit & 1) == 1, 1.0, -1.0) for bit in range(3)]
    d = (e[0] * v[0] + e[1] * v[1] + e[2] * v[2]) * ALONG
    return [
        COS * v[i]
        + e[i] * d
        + ACROSS * (e[(i + 1) % 3] * v[(i + 2) % 3] - e[(i + 2) % 3] * v[(i + 1) % 3])
        for i in range(3)
    ]


def scatter(values, ids, rows, counted, lanes):
    low = (ids & (LANES - 1)).astype(jnp.float32)
    line = (ids >> 7).astype(jnp.float32)
    parts = [split(x) for x in values]
    parts = [p[0] for p in parts] + [p[1] for p in parts]
    spots = places(rows)
    one, zero = jnp.asarray(1, jnp.bfloat16), jnp.asarray(0, jnp.bfloat16)
    left, right = [], []
    for j in range(8):
        mask = spots == narrow(line[j : j + 1], rows)
        lines = [jnp.where(mask, narrow(x[j : j + 1], rows), zero) for x in parts]
        if counted:
            lines.append(jnp.where(mask, one, zero))
        left.append(jnp.concatenate(lines, axis=0))
        right.append(one_hot(low[j : j + 1], lanes))
    return add_up(jnp.concatenate(left, axis=1), jnp.concatenate(right, axis=1))


def mean_of(total):
    return (total[0:96] + total[96:192]) / jnp.maximum(
        jnp.concatenate([total[192:224]] * 3, axis=0), 1.0
    )


def cell_table(mean, axis):
    m = [mean[32 * i : 32 * i + 32] for i in range(3)]
    turned = rotate(axis, m)
    offset = jnp.concatenate([m[i] - turned[i] for i in range(3)], axis=0)
    high, low = split(offset)
    high = jnp.concatenate([high, axis.astype(jnp.float32)], axis=0)
    low = jnp.concatenate([low, jnp.zeros_like(m[0])], axis=0)
    return jnp.concatenate([high, low], axis=1).astype(jnp.bfloat16)


def pick(table, ids, rows, lanes):
    low = (ids & (LANES - 1)).astype(jnp.float32)
    line = ids >> 7
    spots = lax.broadcasted_iota(jnp.int32, (rows, LANES), 0)
    count = table.shape[0] // rows
    parts = [[] for _ in range(count)]
    for j in range(0, 8, 2):
        hot = jnp.concatenate([one_hot(low[j + k : j + k + 1], lanes) for k in range(2)], axis=1)
        wide = jnp.dot(
            table, jnp.concatenate([hot, hot], axis=0), preferred_element_type=jnp.float32
        )
        for k in range(2):
            mask = spots == jnp.broadcast_to(line[j + k : j + k + 1], (rows, LANES))
            for f in range(count):
                found = jnp.zeros((8, LANES), jnp.float32)
                for row in range(0, rows, 8):
                    at = slice(rows * f + row, rows * f + row + 8)
                    found = jnp.where(
                        mask[row : row + 8], wide[at, k * LANES : (k + 1) * LANES], found
                    )
                parts[f].append(found)
    return [fold(p) for p in parts]


def collide(table, cells, v, lanes):
    picked = pick(table, cells, 32, lanes)
    turned = rotate(picked[3].astype(jnp.int32), v)
    return [turned[i] + picked[i] for i in range(3)]


def sum_kernel(low, high, ends, v_ref, cells_ref, *refs):
    done_ref, out_ref = (None, refs[-1]) if low == 0 else (refs[0], refs[-1])
    shape = (224, LANES)

    def step(i, total):
        lanes = places(LANES)
        for part in range(UNROLL):
            at = pl.ds(pl.multiple_of((i * UNROLL + part) * 8, 8), 8)
            v = [v_ref[at, c, :] for c in range(3)]
            total += scatter(v, cells_ref[at, 0, :], 32, True, lanes)
        return total

    total = jnp.zeros(shape, jnp.float32) if done_ref is None else done_ref[...]
    total = lax.fori_loop(low, high, step, total)
    out_ref[...] = mean_of(total) if ends else total


def turn_kernel(v_ref, cells_ref, mean_ref, axis_ref, out_ref, next_ref, total, table):
    total[...] = jnp.zeros_like(total)
    table[...] = cell_table(mean_ref[...], axis_ref[...])

    def step(i, carry):
        lanes = places(LANES)
        added = 0.0
        for part in range(UNROLL):
            at = pl.ds(pl.multiple_of((i * UNROLL + part) * 8, 8), 8)
            v = [v_ref[at, c, :] for c in range(3)]
            new = collide(table[...], cells_ref[at, 0, :], v, lanes)
            for c in range(3):
                out_ref[c, at, :] = new[c]
            added += scatter(new, cells_ref[at, 1, :], 32, True, lanes)
        total[...] += added
        return carry

    lax.fori_loop(0, v_ref.shape[0] // (8 * UNROLL), step, 0)
    next_ref[...] = mean_of(total[...])


def leave(low, high, v_ref, cells_ref, mean_ref, axis_ref, dir_ref, slot_ref, new_ref, first, moved, table):
    table[...] = cell_table(mean_ref[...], axis_ref[...])

    def step(i, carry):
        lanes = places(LANES)
        added = 0.0
        for part in range(UNROLL):
            line = pl.multiple_of((i * UNROLL + part) * 8, 8)
            at = pl.ds(line, 8)
            v = [v_ref[c, at, :] for c in range(3)]
            new = collide(table[...], cells_ref[at, 1, :], v, lanes)
            to = pl.ds(pl.multiple_of(line - first, 8), 8)
            for c in range(3):
                new_ref[c, to, :] = new[c]
            code = dir_ref[at, :]
            key = jnp.where(code > 0, (code - 1) * 256 + slot_ref[at, :], 4096)
            added += scatter(new, key, 16, False, lanes)
        moved[...] += added
        return carry

    lax.fori_loop(low, high, step, 0)


def part_kernel(low, high, *refs):
    inputs, refs = refs[:6], refs[6:]
    new_ref, moved_ref, table = refs[-3:]
    moved_ref[...] = jnp.zeros_like(moved_ref) if low == 0 else refs[0][...]
    leave(low, high, *inputs, new_ref, low * 8 * UNROLL, moved_ref, table)


def places_of(colloid):
    owner = colloid // COLLOIDS_PER_UNIT
    code = jnp.zeros_like(colloid)
    stride = 1
    for axis, up in (("gz", 5), ("gy", 3), ("gx", 1)):
        size = lax.axis_size(axis)
        apart = (owner // stride - lax.axis_index(axis) + size) % size
        code = jnp.where(apart == 1, up, jnp.where(apart == size - 1, up + 1, code))
        stride *= size
    return code * COLLOIDS_PER_UNIT + colloid % COLLOIDS_PER_UNIT


def last_kernel(low, high, *refs):
    inputs, refs = refs[:6], refs[6:]
    before_ref, parts, refs = refs[0], refs[1:3], refs[3:]
    particle_ref, colloid_ref, weight_ref = refs[:3]
    faces = refs[3:5]
    kept_ref, own_ref, *outs = refs[-11:-3]
    moved, table, held = refs[-3:]
    dir_ref = inputs[4]
    moved[...] = before_ref[...]
    start = 0
    for part in parts:
        held[:, start : start + part.shape[1], :] = part[...]
        start += part.shape[1]
    leave(low, high, *inputs, held, 0, moved, table)
    for number, out in enumerate(outs):
        for c in range(3):
            at = 16 * c + 2 * number
            out[2 * c : 2 * c + 2, :] = moved[at : at + 2, :] + moved[48 + at : 50 + at, :]

    def keep(i, carry):
        line = pl.multiple_of(i * 8, 8)
        at = pl.ds(line, 8)
        stays = dir_ref[at, :] == 0
        for c in range(3):
            kept = jnp.where(stays, held[c, at, :], 0.0)
            for j in range(8):
                kept_ref[c : c + 1, pl.ds((line + j) * LANES, LANES)] = kept[j : j + 1]
        return carry

    lines = held.shape[1]
    lax.fori_loop(0, lines // 8, keep, 0, unroll=4)
    high_part, low_part = split(held[...].reshape(3 * lines, LANES))
    wide = jnp.concatenate([high_part, low_part], axis=1).astype(jnp.bfloat16)
    lanes = places(LANES)
    force = jnp.zeros((128, LANES), jnp.float32)
    for part in range(particle_ref.shape[0] // 8):
        at = slice(8 * part, 8 * part + 8)
        weight = weight_ref[at, :]
        terms = [weight * x for x in pick(wide, particle_ref[at, :], lines, lanes)] + [weight]
        force = force + scatter(terms, places_of(colloid_ref[at, :]), 16, False, lanes)
    force = force[0:64] + force[64:128]
    for f in range(4):
        own_ref[2 * f : 2 * f + 2, :] = force[16 * f : 16 * f + 2]
        for number, out in enumerate(outs):
            at = 16 * f + 2 * number + 2
            out[6 + 2 * f : 8 + 2 * f, :] = force[at : at + 2]
    for out, face in zip(outs[4:], faces):
        out[14:15, :] = face[...]


def prepare_kernel(shift_ref, axis_ref, sign_ref, first_ref, last_ref, rise_ref, fall_ref):
    rows = lax.broadcasted_iota(jnp.int32, (8, LANES), 0)
    sign = jnp.zeros((8, LANES), jnp.int32)
    for dim in range(3):
        sign = jnp.where(rows == dim, shift_ref[0, dim], sign)
    sign_ref[...] = sign
    up = jnp.full(rise_ref.shape, shift_ref[0, 0], jnp.int32) > 0
    rise_ref[...] = jnp.where(up, axis_ref[0], axis_ref[1])
    fall_ref[...] = jnp.where(up, axis_ref[1], axis_ref[0])
    first_ref[...] = rise_ref[0 : first_ref.shape[0], :]
    last_ref[...] = fall_ref[fall_ref.shape[0] - last_ref.shape[0] :, :]


def finish_kernel(sign_ref, mean_ref, own_ref, speed_ref, *refs):
    came, (mean_out, moved_out, force_out) = refs[:6], refs[6:]
    mean = mean_ref[...]
    rows = mean.shape[0]
    sides = [jnp.broadcast_to(x[14:15, :], (8, LANES)).T[:rows, 0:1] for x in came[4:]]
    lane = lax.broadcasted_iota(jnp.int32, mean.shape, 1)
    ahead_mean = jnp.where(lane == LANES - 1, sides[1], pltpu.roll(mean, LANES - 1, 1))
    behind_mean = jnp.where(lane == 0, sides[0], pltpu.roll(mean, 1, 1))
    up = jnp.broadcast_to(sign_ref[2:3, :], mean.shape) > 0
    mean_out[...] = jnp.where(up, ahead_mean, behind_mean)
    total = own_ref[...]
    for x in came:
        total = total + x[6:14, :]
    for c in range(3):
        pieces = []
        for x in came:
            pieces += [x[2 * c : 2 * c + 1, :], x[2 * c + 1 : 2 * c + 2, : CAP - LANES]]
        moved_out[c : c + 1, :] = jnp.concatenate(pieces, axis=1)
        for half in range(2):
            at = slice(half * LANES, half * LANES + LANES)
            weight = total[6 + half : 7 + half]
            rest = total[2 * c + half : 2 * c + half + 1] - weight * speed_ref[c : c + 1, at]
            force_out[c : c + 1, at] = rest / jnp.maximum(weight, 1.0)


def call(kernel, name, outs, scratch, flops, args, scalars=0):
    vmem = pl.BlockSpec(memory_space=pltpu.VMEM)
    smem = pl.BlockSpec(memory_space=pltpu.SMEM)
    outs = [out if hasattr(out, "dtype") else jax.ShapeDtypeStruct(out, jnp.float32) for out in outs]
    return pl.pallas_call(
        kernel,
        name=name,
        out_shape=outs,
        in_specs=[smem] * scalars + [vmem] * (len(args) - scalars),
        out_specs=[vmem] * len(outs),
        scratch_shapes=scratch,
        compiler_params=pltpu.CompilerParams(vmem_limit_bytes=VMEM_LIMIT),
        cost_estimate=pl.CostEstimate(flops=flops, bytes_accessed=2 << 20, transcendentals=0),
    )(*args)


def ring(axis, by):
    count = lax.axis_size(axis)
    return [(i, (i + by) % count) for i in range(count)]


def first(x, dim):
    return lax.slice_in_dim(x, 0, 1, axis=dim)


def last(x, dim):
    return lax.slice_in_dim(x, x.shape[dim] - 1, x.shape[dim], axis=dim)


def ahead(x, rim, dim):
    return jnp.concatenate([lax.slice_in_dim(x, 1, x.shape[dim], axis=dim), rim], axis=dim)


def behind(x, rim, dim):
    return jnp.concatenate([rim, lax.slice_in_dim(x, 0, x.shape[dim] - 1, axis=dim)], axis=dim)


def axis_round(rise, fall, sent, dim, axis):
    upper = lax.ppermute(sent[0], axis, ring(axis, -1))
    lower = lax.ppermute(sent[1], axis, ring(axis, 1))
    return ahead(rise, upper, dim), behind(fall, lower, dim), (upper, lower)


def mean_round(mean, up, dim, axis):
    lower = lax.ppermute(last(mean, dim + 1), axis, ring(axis, 1))
    upper = lax.ppermute(first(mean, dim + 1), axis, ring(axis, -1))
    mean = jnp.where(up, ahead(mean, upper, dim + 1), behind(mean, lower, dim + 1))
    return mean, (upper, lower)


def body(
    velocities,
    particle_cells,
    grid_shift,
    axis_index,
    migrate_dir,
    migrate_slot,
    contact_colloid,
    contact_particle,
    contact_weight,
    colloid_velocity,
):
    particles = velocities.shape[1]
    cells_x, cells_y, cells_z = axis_index.shape[1:]
    lines = particles // LANES
    steps = lines // (8 * UNROLL)
    cuts = (0, steps * 3 // 10, steps * 6 // 10, steps)
    spans = tuple(zip(cuts[:-1], cuts[1:]))
    velocity = velocities.reshape(3, lines, LANES).transpose(1, 0, 2)
    cells = particle_cells.reshape(2, lines, LANES).transpose(1, 0, 2)
    total = pltpu.VMEM((224, LANES), jnp.float32)
    table = pltpu.VMEM((128, 256), jnp.bfloat16)
    pair_flops = 2 * 224 * 128 * particles

    plane, cells_all = cells_y, cells_x * cells_y
    whole = jax.ShapeDtypeStruct((cells_all, cells_z), jnp.int32)
    rim = jax.ShapeDtypeStruct((plane, cells_z), jnp.int32)
    sign, first_rim, last_rim, rise, fall = call(
        prepare_kernel,
        "prepare",
        [jax.ShapeDtypeStruct((8, LANES), jnp.int32), rim, rim, whole, whole],
        [],
        1 << 16,
        (grid_shift, axis_index.reshape(2, cells_all, cells_z)),
        scalars=1,
    )
    up = [sign[dim, 0] > 0 for dim in range(3)]
    rise = rise.reshape(cells_x, cells_y, cells_z)
    fall = fall.reshape(cells_x, cells_y, cells_z)
    sent = (first_rim[None], last_rim[None])
    summed = ()
    for dim, axis in enumerate(("gx", "gy", "gz")):
        rise, fall, rims = axis_round(rise, fall, sent, dim, axis)
        axes = (jnp.where(up[dim], rise, fall), jnp.where(up[dim], fall, rise))
        if dim < 2:
            rise = jnp.where(up[dim + 1], axes[0], axes[1])
            fall = jnp.where(up[dim + 1], axes[1], axes[0])
            sent = (first(rise, dim + 1), last(fall, dim + 1))
        low, high = spans[dim]
        ends = dim == 2
        (result,) = call(
            functools.partial(sum_kernel, low, high, ends),
            "sums_%d" % dim,
            [(96 if ends else 224, LANES)],
            [],
            pair_flops // 3,
            (velocity, cells) + summed,
        )
        summed = (result,) + rims
    mean0 = result
    axes = [x.reshape(cells_all, cells_z) for x in axes]
    moving, mean1 = call(
        turn_kernel,
        "turn",
        [(3, lines, LANES), (96, LANES)],
        [total, table],
        2 * pair_flops,
        (velocity, cells, mean0, axes[0]),
    )
    shared = (
        moving,
        cells,
        mean1,
        axes[1],
        migrate_dir.reshape(lines, LANES),
        migrate_slot.reshape(lines, LANES),
    )
    mean = mean1.reshape(3, cells_x, cells_y, cells_z)
    tied = ()
    parts = []
    for dim, axis in enumerate(("gx", "gy")):
        mean, rims = mean_round(mean, up[dim], dim, axis)
        low, high = spans[dim]
        part, moved = call(
            functools.partial(part_kernel, low, high),
            "part_%d" % dim,
            [(3, (high - low) * 8 * UNROLL, LANES), (96, LANES)],
            [table],
            pair_flops // 2,
            shared + tied,
        )
        parts.append(part)
        tied = (moved,) + rims
    faces = [
        jnp.pad(x.reshape(1, -1), ((0, 0), (0, LANES - 3 * cells_all)))
        for x in (last(mean, 3), first(mean, 3))
    ]
    low, high = spans[2]
    kept, own, *blocks = call(
        functools.partial(last_kernel, low, high),
        "last",
        [(3, particles + 6 * CAP), (8, LANES)] + [(14, LANES)] * 4 + [(15, LANES)] * 2,
        [
            pltpu.VMEM((96, LANES), jnp.float32),
            table,
            pltpu.VMEM((3, lines, LANES), jnp.float32),
        ],
        pair_flops,
        shared
        + (moved, *parts)
        + (
            contact_particle.reshape(-1, LANES),
            contact_colloid.reshape(-1, LANES),
            contact_weight.reshape(-1, LANES),
            *faces,
        )
        + rims,
    )
    came = []
    for number, block in enumerate(blocks):
        axis, by = ("gx", "gy", "gz")[number // 2], 1 - 2 * (number % 2)
        came.append(lax.ppermute(block, axis, ring(axis, by)))
    mean, arrivals, colloid_force = call(
        finish_kernel,
        "finish",
        [(3 * cells_all, cells_z), (3, 6 * CAP), colloid_velocity.shape],
        [],
        1 << 20,
        (sign, mean.reshape(3 * cells_all, cells_z), own, colloid_velocity, *came),
    )
    mean = mean.reshape(3, cells_x, cells_y, cells_z)
    migrated = lax.dynamic_update_slice(kept, arrivals, (0, particles))
    return (mean, migrated, colloid_force)


def solution(mesh):
    flat = P(("gx", "gy", "gz"))
    tall = P(None, ("gx", "gy", "gz"))
    grid = P(None, "gx", "gy", "gz")
    return jax.shard_map(
        body,
        mesh=mesh,
        in_specs=(tall, tall, P(), grid, flat, flat, flat, flat, flat, tall),
        out_specs=(grid, tall, tall),
        check_vma=False,
    )
```

```python
import functools
import math

import jax
import jax.numpy as jnp
from jax import lax
from jax.experimental import pallas as pl
from jax.experimental.pallas import tpu as pltpu
from jax.sharding import PartitionSpec as P

COLLOIDS_PER_UNIT = 256
CAP = 160
LANES = 128
UNROLL = 4
ANGLE = 130.0 * math.pi / 180.0
COS = math.cos(ANGLE)
ALONG = (1.0 - math.cos(ANGLE)) / 3.0
ACROSS = math.sin(ANGLE) / math.sqrt(3.0)
VMEM_LIMIT = 48 << 20


def split(x):
    high = x.astype(jnp.bfloat16).astype(jnp.float32)
    return high, x - high


def places(rows):
    return lax.broadcasted_iota(jnp.int32, (rows, LANES), 0).astype(jnp.float32).astype(jnp.bfloat16)


def narrow(row, rows):
    part = jnp.broadcast_to(row, (16, LANES)).astype(jnp.bfloat16)
    return jnp.concatenate([part] * (rows // 16), axis=0)


def one_hot(row, lanes):
    one, zero = jnp.asarray(1, jnp.bfloat16), jnp.asarray(0, jnp.bfloat16)
    return jnp.where(lanes == narrow(row, LANES), one, zero)


def add_up(left, right):
    return lax.dot_general(
        left, right, (((1,), (1,)), ((), ())), preferred_element_type=jnp.float32
    )


def fold(parts):
    rows = lax.broadcasted_iota(jnp.int32, parts[0].shape, 0)
    step = 1
    while len(parts) > 1:
        low = (rows & step) == 0
        parts = [
            jnp.where(low, p, q) + pltpu.roll(jnp.where(low, q, p), step, 0)
            for p, q in zip(parts[0::2], parts[1::2])
        ]
        step *= 2
    return parts[0]


def rotate(axis, v):
    e = [jnp.where((axis >> bit & 1) == 1, 1.0, -1.0) for bit in range(3)]
    d = (e[0] * v[0] + e[1] * v[1] + e[2] * v[2]) * ALONG
    return [
        COS * v[i]
        + e[i] * d
        + ACROSS * (e[(i + 1) % 3] * v[(i + 2) % 3] - e[(i + 2) % 3] * v[(i + 1) % 3])
        for i in range(3)
    ]


def scatter(values, ids, rows, counted, lanes):
    low = (ids & (LANES - 1)).astype(jnp.float32)
    line = (ids >> 7).astype(jnp.float32)
    parts = [split(x) for x in values]
    parts = [p[0] for p in parts] + [p[1] for p in parts]
    spots = places(rows)
    one, zero = jnp.asarray(1, jnp.bfloat16), jnp.asarray(0, jnp.bfloat16)
    left, right = [], []
    for j in range(8):
        mask = spots == narrow(line[j : j + 1], rows)
        lines = [jnp.where(mask, narrow(x[j : j + 1], rows), zero) for x in parts]
        if counted:
            lines.append(jnp.where(mask, one, zero))
        left.append(jnp.concatenate(lines, axis=0))
        right.append(one_hot(low[j : j + 1], lanes))
    return add_up(jnp.concatenate(left, axis=1), jnp.concatenate(right, axis=1))


def mean_of(total):
    return (total[0:96] + total[96:192]) / jnp.maximum(
        jnp.concatenate([total[192:224]] * 3, axis=0), 1.0
    )


def cell_table(mean, axis):
    m = [mean[32 * i : 32 * i + 32] for i in range(3)]
    turned = rotate(axis, m)
    offset = jnp.concatenate([m[i] - turned[i] for i in range(3)], axis=0)
    high, low = split(offset)
    high = jnp.concatenate([high, axis.astype(jnp.float32)], axis=0)
    low = jnp.concatenate([low, jnp.zeros_like(m[0])], axis=0)
    return jnp.concatenate([high, low], axis=1).astype(jnp.bfloat16)


def pick(table, ids, rows, lanes):
    low = (ids & (LANES - 1)).astype(jnp.float32)
    line = ids >> 7
    spots = lax.broadcasted_iota(jnp.int32, (rows, LANES), 0)
    count = table.shape[0] // rows
    parts = [[] for _ in range(count)]
    for j in range(0, 8, 2):
        hot = jnp.concatenate([one_hot(low[j + k : j + k + 1], lanes) for k in range(2)], axis=1)
        wide = jnp.dot(
            table, jnp.concatenate([hot, hot], axis=0), preferred_element_type=jnp.float32
        )
        for k in range(2):
            mask = spots == jnp.broadcast_to(line[j + k : j + k + 1], (rows, LANES))
            for f in range(count):
                found = jnp.zeros((8, LANES), jnp.float32)
                for row in range(0, rows, 8):
                    at = slice(rows * f + row, rows * f + row + 8)
                    found = jnp.where(
                        mask[row : row + 8], wide[at, k * LANES : (k + 1) * LANES], found
                    )
                parts[f].append(found)
    return [fold(p) for p in parts]


def collide(table, cells, v, lanes):
    picked = pick(table, cells, 32, lanes)
    turned = rotate(picked[3].astype(jnp.int32), v)
    return [turned[i] + picked[i] for i in range(3)]


def sum_kernel(low, high, ends, v_ref, cells_ref, *refs):
    done_ref, out_ref = (None, refs[-1]) if low == 0 else (refs[0], refs[-1])
    shape = (224, LANES)

    def step(i, total):
        lanes = places(LANES)
        for part in range(UNROLL):
            at = pl.ds(pl.multiple_of((i * UNROLL + part) * 8, 8), 8)
            v = [v_ref[at, c, :] for c in range(3)]
            total += scatter(v, cells_ref[at, 0, :], 32, True, lanes)
        return total

    total = jnp.zeros(shape, jnp.float32) if done_ref is None else done_ref[...]
    total = lax.fori_loop(low, high, step, total)
    out_ref[...] = mean_of(total) if ends else total


def turn_kernel(v_ref, cells_ref, mean_ref, axis_ref, out_ref, next_ref, total, table):
    total[...] = jnp.zeros_like(total)
    table[...] = cell_table(mean_ref[...], axis_ref[...])

    def step(i, carry):
        lanes = places(LANES)
        added = 0.0
        for part in range(UNROLL):
            at = pl.ds(pl.multiple_of((i * UNROLL + part) * 8, 8), 8)
            v = [v_ref[at, c, :] for c in range(3)]
            new = collide(table[...], cells_ref[at, 0, :], v, lanes)
            for c in range(3):
                out_ref[c, at, :] = new[c]
            added += scatter(new, cells_ref[at, 1, :], 32, True, lanes)
        total[...] += added
        return carry

    lax.fori_loop(0, v_ref.shape[0] // (8 * UNROLL), step, 0)
    next_ref[...] = mean_of(total[...])


def leave(low, high, v_ref, cells_ref, mean_ref, axis_ref, dir_ref, slot_ref, new_ref, first, moved, table):
    table[...] = cell_table(mean_ref[...], axis_ref[...])

    def step(i, carry):
        lanes = places(LANES)
        added = 0.0
        for part in range(UNROLL):
            line = pl.multiple_of((i * UNROLL + part) * 8, 8)
            at = pl.ds(line, 8)
            v = [v_ref[c, at, :] for c in range(3)]
            new = collide(table[...], cells_ref[at, 1, :], v, lanes)
            to = pl.ds(pl.multiple_of(line - first, 8), 8)
            for c in range(3):
                new_ref[c, to, :] = new[c]
            code = dir_ref[at, :]
            key = jnp.where(code > 0, (code - 1) * 256 + slot_ref[at, :], 4096)
            added += scatter(new, key, 16, False, lanes)
        moved[...] += added
        return carry

    lax.fori_loop(low, high, step, 0)


def part_kernel(low, high, *refs):
    inputs, refs = refs[:6], refs[6:]
    new_ref, moved_ref, table = refs[-3:]
    moved_ref[...] = jnp.zeros_like(moved_ref) if low == 0 else refs[0][...]
    leave(low, high, *inputs, new_ref, low * 8 * UNROLL, moved_ref, table)


def places_of(colloid):
    owner = colloid // COLLOIDS_PER_UNIT
    code = jnp.zeros_like(colloid)
    stride = 1
    for axis, up in (("gz", 5), ("gy", 3), ("gx", 1)):
        size = lax.axis_size(axis)
        apart = (owner // stride - lax.axis_index(axis) + size) % size
        code = jnp.where(apart == 1, up, jnp.where(apart == size - 1, up + 1, code))
        stride *= size
    return code * COLLOIDS_PER_UNIT + colloid % COLLOIDS_PER_UNIT


def last_kernel(low, high, *refs):
    inputs, refs = refs[:6], refs[6:]
    before_ref, parts, refs = refs[0], refs[1:3], refs[3:]
    particle_ref, colloid_ref, weight_ref = refs[:3]
    faces = refs[3:5]
    kept_ref, own_ref, *outs = refs[-11:-3]
    moved, table, held = refs[-3:]
    dir_ref = inputs[4]
    moved[...] = before_ref[...]
    start = 0
    for part in parts:
        held[:, start : start + part.shape[1], :] = part[...]
        start += part.shape[1]
    leave(low, high, *inputs, held, 0, moved, table)
    for number, out in enumerate(outs):
        for c in range(3):
            at = 16 * c + 2 * number
            out[2 * c : 2 * c + 2, :] = moved[at : at + 2, :] + moved[48 + at : 50 + at, :]

    def keep(i, carry):
        line = pl.multiple_of(i * 8, 8)
        at = pl.ds(line, 8)
        stays = dir_ref[at, :] == 0
        for c in range(3):
            kept = jnp.where(stays, held[c, at, :], 0.0)
            for j in range(8):
                kept_ref[c : c + 1, pl.ds((line + j) * LANES, LANES)] = kept[j : j + 1]
        return carry

    lines = held.shape[1]
    lax.fori_loop(0, lines // 8, keep, 0, unroll=4)
    high_part, low_part = split(held[...].reshape(3 * lines, LANES))
    wide = jnp.concatenate([high_part, low_part], axis=1).astype(jnp.bfloat16)
    lanes = places(LANES)
    force = jnp.zeros((128, LANES), jnp.float32)
    for part in range(particle_ref.shape[0] // 8):
        at = slice(8 * part, 8 * part + 8)
        weight = weight_ref[at, :]
        terms = [weight * x for x in pick(wide, particle_ref[at, :], lines, lanes)] + [weight]
        force = force + scatter(terms, places_of(colloid_ref[at, :]), 16, False, lanes)
    force = force[0:64] + force[64:128]
    for f in range(4):
        own_ref[2 * f : 2 * f + 2, :] = force[16 * f : 16 * f + 2]
        for number, out in enumerate(outs):
            at = 16 * f + 2 * number + 2
            out[6 + 2 * f : 8 + 2 * f, :] = force[at : at + 2]
    for out, face in zip(outs[4:], faces):
        out[14:15, :] = face[...]


def prepare_kernel(shift_ref, axis_ref, sign_ref, first_ref, last_ref, rise_ref, fall_ref):
    rows = lax.broadcasted_iota(jnp.int32, (8, LANES), 0)
    sign = jnp.zeros((8, LANES), jnp.int32)
    for dim in range(3):
        sign = jnp.where(rows == dim, shift_ref[0, dim], sign)
    sign_ref[...] = sign
    up = jnp.full(rise_ref.shape, shift_ref[0, 0], jnp.int32) > 0
    rise_ref[...] = jnp.where(up, axis_ref[0], axis_ref[1])
    fall_ref[...] = jnp.where(up, axis_ref[1], axis_ref[0])
    first_ref[...] = rise_ref[0 : first_ref.shape[0], :]
    last_ref[...] = fall_ref[fall_ref.shape[0] - last_ref.shape[0] :, :]


def finish_kernel(sign_ref, mean_ref, own_ref, speed_ref, *refs):
    came, (mean_out, moved_out, force_out) = refs[:6], refs[6:]
    mean = mean_ref[...]
    rows = mean.shape[0]
    sides = [jnp.broadcast_to(x[14:15, :], (8, LANES)).T[:rows, 0:1] for x in came[4:]]
    lane = lax.broadcasted_iota(jnp.int32, mean.shape, 1)
    ahead_mean = jnp.where(lane == LANES - 1, sides[1], pltpu.roll(mean, LANES - 1, 1))
    behind_mean = jnp.where(lane == 0, sides[0], pltpu.roll(mean, 1, 1))
    up = jnp.broadcast_to(sign_ref[2:3, :], mean.shape) > 0
    mean_out[...] = jnp.where(up, ahead_mean, behind_mean)
    total = own_ref[...]
    for x in came:
        total = total + x[6:14, :]
    for c in range(3):
        pieces = []
        for x in came:
            pieces += [x[2 * c : 2 * c + 1, :], x[2 * c + 1 : 2 * c + 2, : CAP - LANES]]
        moved_out[c : c + 1, :] = jnp.concatenate(pieces, axis=1)
        for half in range(2):
            at = slice(half * LANES, half * LANES + LANES)
            weight = total[6 + half : 7 + half]
            rest = total[2 * c + half : 2 * c + half + 1] - weight * speed_ref[c : c + 1, at]
            force_out[c : c + 1, at] = rest / jnp.maximum(weight, 1.0)


def call(kernel, name, outs, scratch, flops, args, scalars=0):
    vmem = pl.BlockSpec(memory_space=pltpu.VMEM)
    smem = pl.BlockSpec(memory_space=pltpu.SMEM)
    outs = [out if hasattr(out, "dtype") else jax.ShapeDtypeStruct(out, jnp.float32) for out in outs]
    return pl.pallas_call(
        kernel,
        name=name,
        out_shape=outs,
        in_specs=[smem] * scalars + [vmem] * (len(args) - scalars),
        out_specs=[vmem] * len(outs),
        scratch_shapes=scratch,
        compiler_params=pltpu.CompilerParams(vmem_limit_bytes=VMEM_LIMIT),
        cost_estimate=pl.CostEstimate(flops=flops, bytes_accessed=2 << 20, transcendentals=0),
    )(*args)


def ring(axis, by):
    count = lax.axis_size(axis)
    return [(i, (i + by) % count) for i in range(count)]


def first(x, dim):
    return lax.slice_in_dim(x, 0, 1, axis=dim)


def last(x, dim):
    return lax.slice_in_dim(x, x.shape[dim] - 1, x.shape[dim], axis=dim)


def ahead(x, rim, dim):
    return jnp.concatenate([lax.slice_in_dim(x, 1, x.shape[dim], axis=dim), rim], axis=dim)


def behind(x, rim, dim):
    return jnp.concatenate([rim, lax.slice_in_dim(x, 0, x.shape[dim] - 1, axis=dim)], axis=dim)


def axis_round(rise, fall, sent, dim, axis):
    upper = lax.ppermute(sent[0], axis, ring(axis, -1))
    lower = lax.ppermute(sent[1], axis, ring(axis, 1))
    return ahead(rise, upper, dim), behind(fall, lower, dim), (upper, lower)


def mean_round(mean, up, dim, axis):
    lower = lax.ppermute(last(mean, dim + 1), axis, ring(axis, 1))
    upper = lax.ppermute(first(mean, dim + 1), axis, ring(axis, -1))
    mean = jnp.where(up, ahead(mean, upper, dim + 1), behind(mean, lower, dim + 1))
    return mean, (upper, lower)


def body(
    velocities,
    particle_cells,
    grid_shift,
    axis_index,
    migrate_dir,
    migrate_slot,
    contact_colloid,
    contact_particle,
    contact_weight,
    colloid_velocity,
):
    particles = velocities.shape[1]
    cells_x, cells_y, cells_z = axis_index.shape[1:]
    lines = particles // LANES
    steps = lines // (8 * UNROLL)
    cuts = (0, steps * 3 // 10, steps * 6 // 10, steps)
    spans = tuple(zip(cuts[:-1], cuts[1:]))
    velocity = velocities.reshape(3, lines, LANES).transpose(1, 0, 2)
    cells = particle_cells.reshape(2, lines, LANES).transpose(1, 0, 2)
    total = pltpu.VMEM((224, LANES), jnp.float32)
    table = pltpu.VMEM((128, 256), jnp.bfloat16)
    pair_flops = 2 * 224 * 128 * particles

    plane, cells_all = cells_y, cells_x * cells_y
    whole = jax.ShapeDtypeStruct((cells_all, cells_z), jnp.int32)
    rim = jax.ShapeDtypeStruct((plane, cells_z), jnp.int32)
    sign, first_rim, last_rim, rise, fall = call(
        prepare_kernel,
        "prepare",
        [jax.ShapeDtypeStruct((8, LANES), jnp.int32), rim, rim, whole, whole],
        [],
        1 << 16,
        (grid_shift, axis_index.reshape(2, cells_all, cells_z)),
        scalars=1,
    )
    up = [sign[dim] > 0 for dim in range(3)]
    rise = rise.reshape(cells_x, cells_y, cells_z)
    fall = fall.reshape(cells_x, cells_y, cells_z)
    sent = (first_rim[None], last_rim[None])
    summed = ()
    for dim, axis in enumerate(("gx", "gy", "gz")):
        rise, fall, rims = axis_round(rise, fall, sent, dim, axis)
        axes = (jnp.where(up[dim], rise, fall), jnp.where(up[dim], fall, rise))
        if dim < 2:
            rise = jnp.where(up[dim + 1], axes[0], axes[1])
            fall = jnp.where(up[dim + 1], axes[1], axes[0])
            sent = (first(rise, dim + 1), last(fall, dim + 1))
        low, high = spans[dim]
        ends = dim == 2
        (result,) = call(
            functools.partial(sum_kernel, low, high, ends),
            "sums_%d" % dim,
            [(96 if ends else 224, LANES)],
            [],
            pair_flops // 3,
            (velocity, cells) + summed,
        )
        summed = (result,) + rims
    mean0 = result
    axes = [x.reshape(cells_all, cells_z) for x in axes]
    moving, mean1 = call(
        turn_kernel,
        "turn",
        [(3, lines, LANES), (96, LANES)],
        [total, table],
        2 * pair_flops,
        (velocity, cells, mean0, axes[0]),
    )
    shared = (
        moving,
        cells,
        mean1,
        axes[1],
        migrate_dir.reshape(lines, LANES),
        migrate_slot.reshape(lines, LANES),
    )
    mean = mean1.reshape(3, cells_x, cells_y, cells_z)
    tied = ()
    parts = []
    for dim, axis in enumerate(("gx", "gy")):
        mean, rims = mean_round(mean, up[dim], dim, axis)
        low, high = spans[dim]
        part, moved = call(
            functools.partial(part_kernel, low, high),
            "part_%d" % dim,
            [(3, (high - low) * 8 * UNROLL, LANES), (96, LANES)],
            [table],
            pair_flops // 2,
            shared + tied,
        )
        parts.append(part)
        tied = (moved,) + rims
    faces = [
        jnp.pad(x.reshape(1, -1), ((0, 0), (0, LANES - 3 * cells_all)))
        for x in (last(mean, 3), first(mean, 3))
    ]
    low, high = spans[2]
    kept, own, *blocks = call(
        functools.partial(last_kernel, low, high),
        "last",
        [(3, particles + 6 * CAP), (8, LANES)] + [(14, LANES)] * 4 + [(15, LANES)] * 2,
        [
            pltpu.VMEM((96, LANES), jnp.float32),
            table,
            pltpu.VMEM((3, lines, LANES), jnp.float32),
        ],
        pair_flops,
        shared
        + (moved, *parts)
        + (
            contact_particle.reshape(-1, LANES),
            contact_colloid.reshape(-1, LANES),
            contact_weight.reshape(-1, LANES),
            *faces,
        )
        + rims,
    )
    came = []
    for number, block in enumerate(blocks):
        axis, by = ("gx", "gy", "gz")[number // 2], 1 - 2 * (number % 2)
        came.append(lax.ppermute(block, axis, ring(axis, by)))
    mean, arrivals, colloid_force = call(
        finish_kernel,
        "finish",
        [(3 * cells_all, cells_z), (3, 6 * CAP), colloid_velocity.shape],
        [],
        1 << 20,
        (sign, mean.reshape(3 * cells_all, cells_z), own, colloid_velocity, *came),
    )
    mean = mean.reshape(3, cells_x, cells_y, cells_z)
    migrated = lax.dynamic_update_slice(kept, arrivals, (0, particles))
    return (mean, migrated, colloid_force)


def solution(mesh):
    flat = P(("gx", "gy", "gz"))
    tall = P(None, ("gx", "gy", "gz"))
    grid = P(None, "gx", "gy", "gz")
    return jax.shard_map(
        body,
        mesh=mesh,
        in_specs=(tall, tall, P(), grid, flat, flat, flat, flat, flat, tall),
        out_specs=(grid, tall, tall),
        check_vma=False,
    )
```

```python
import functools
import math

import jax
import jax.numpy as jnp
from jax import lax
from jax.experimental import pallas as pl
from jax.experimental.pallas import tpu as pltpu
from jax.sharding import PartitionSpec as P

COLLOIDS_PER_UNIT = 256
CAP = 160
LANES = 128
UNROLL = 20
ANGLE = 130.0 * math.pi / 180.0
COS = math.cos(ANGLE)
ALONG = (1.0 - math.cos(ANGLE)) / 3.0
ACROSS = math.sin(ANGLE) / math.sqrt(3.0)
VMEM_LIMIT = 48 << 20


def split(x):
    high = x.astype(jnp.bfloat16).astype(jnp.float32)
    return high, x - high


def places(rows):
    return lax.broadcasted_iota(jnp.int32, (rows, LANES), 0).astype(jnp.float32).astype(jnp.bfloat16)


def narrow(row, rows):
    part = jnp.broadcast_to(row, (16, LANES)).astype(jnp.bfloat16)
    return jnp.concatenate([part] * (rows // 16), axis=0)


def one_hot(row, lanes):
    one, zero = jnp.asarray(1, jnp.bfloat16), jnp.asarray(0, jnp.bfloat16)
    return jnp.where(lanes == narrow(row, LANES), one, zero)


def add_up(left, right):
    return lax.dot_general(
        left, right, (((1,), (1,)), ((), ())), preferred_element_type=jnp.float32
    )


def fold(parts):
    rows = lax.broadcasted_iota(jnp.int32, parts[0].shape, 0)
    step = 1
    while len(parts) > 1:
        low = (rows & step) == 0
        parts = [
            jnp.where(low, p, q) + pltpu.roll(jnp.where(low, q, p), step, 0)
            for p, q in zip(parts[0::2], parts[1::2])
        ]
        step *= 2
    return parts[0]


def rotate(axis, v):
    e = [jnp.where((axis >> bit & 1) == 1, 1.0, -1.0) for bit in range(3)]
    d = (e[0] * v[0] + e[1] * v[1] + e[2] * v[2]) * ALONG
    return [
        COS * v[i]
        + e[i] * d
        + ACROSS * (e[(i + 1) % 3] * v[(i + 2) % 3] - e[(i + 2) % 3] * v[(i + 1) % 3])
        for i in range(3)
    ]


def scatter(values, ids, rows, counted, lanes):
    low = (ids & (LANES - 1)).astype(jnp.float32)
    line = (ids >> 7).astype(jnp.float32)
    parts = [split(x) for x in values]
    parts = [p[0] for p in parts] + [p[1] for p in parts]
    spots = places(rows)
    one, zero = jnp.asarray(1, jnp.bfloat16), jnp.asarray(0, jnp.bfloat16)
    left, right = [], []
    for j in range(8):
        mask = spots == narrow(line[j : j + 1], rows)
        lines = [jnp.where(mask, narrow(x[j : j + 1], rows), zero) for x in parts]
        if counted:
            lines.append(jnp.where(mask, one, zero))
        left.append(jnp.concatenate(lines, axis=0))
        right.append(one_hot(low[j : j + 1], lanes))
    return add_up(jnp.concatenate(left, axis=1), jnp.concatenate(right, axis=1))


def mean_of(total):
    return (total[0:96] + total[96:192]) / jnp.maximum(
        jnp.concatenate([total[192:224]] * 3, axis=0), 1.0
    )


def cell_table(mean, axis):
    m = [mean[32 * i : 32 * i + 32] for i in range(3)]
    turned = rotate(axis, m)
    offset = jnp.concatenate([m[i] - turned[i] for i in range(3)], axis=0)
    high, low = split(offset)
    high = jnp.concatenate([high, axis.astype(jnp.float32)], axis=0)
    low = jnp.concatenate([low, jnp.zeros_like(m[0])], axis=0)
    return jnp.concatenate([high, low], axis=1).astype(jnp.bfloat16)


def pick(table, ids, rows, lanes):
    low = (ids & (LANES - 1)).astype(jnp.float32)
    line = ids >> 7
    spots = lax.broadcasted_iota(jnp.int32, (rows, LANES), 0)
    count = table.shape[0] // rows
    parts = [[] for _ in range(count)]
    for j in range(0, 8, 2):
        hot = jnp.concatenate([one_hot(low[j + k : j + k + 1], lanes) for k in range(2)], axis=1)
        wide = jnp.dot(
            table, jnp.concatenate([hot, hot], axis=0), preferred_element_type=jnp.float32
        )
        for k in range(2):
            mask = spots == jnp.broadcast_to(line[j + k : j + k + 1], (rows, LANES))
            for f in range(count):
                found = jnp.zeros((8, LANES), jnp.float32)
                for row in range(0, rows, 8):
                    at = slice(rows * f + row, rows * f + row + 8)
                    found = jnp.where(
                        mask[row : row + 8], wide[at, k * LANES : (k + 1) * LANES], found
                    )
                parts[f].append(found)
    return [fold(p) for p in parts]


def collide(table, cells, v, lanes):
    picked = pick(table, cells, 32, lanes)
    turned = rotate(picked[3].astype(jnp.int32), v)
    return [turned[i] + picked[i] for i in range(3)]


def sweep(low, high, total, pick_block, add_block):
    count = high - low
    unroll = max(u for u in range(1, UNROLL + 1) if count % u == 0)

    def step(i, carry):
        lanes = places(LANES)
        added, held = 0.0, None
        for part in range(unroll + 1):
            line = pl.multiple_of((low + i * unroll + part) * 8, 8)
            new = pick_block(line, lanes) if part < unroll else None
            if part:
                added += add_block(line - 8, held, lanes)
            held = new
        total[...] += added
        return carry

    lax.fori_loop(0, count // unroll, step, 0)


def rows_at(line):
    return pl.ds(pl.multiple_of(line, 8), 8)


def sum_kernel(low, high, ends, v_ref, cells_ref, *refs):
    out_ref, total = refs[-2:]
    total[...] = jnp.zeros_like(total) if low == 0 else refs[0][...]

    def load(line, lanes):
        return [v_ref[rows_at(line), c, :] for c in range(3)]

    def add(line, v, lanes):
        return scatter(v, cells_ref[rows_at(line), 0, :], 32, True, lanes)

    sweep(low, high, total, load, add)
    out_ref[...] = mean_of(total[...]) if ends else total[...]


def turn_kernel(v_ref, cells_ref, mean_ref, axis_ref, out_ref, next_ref, total, table):
    total[...] = jnp.zeros_like(total)
    table[...] = cell_table(mean_ref[...], axis_ref[...])

    def turn(line, lanes):
        at = rows_at(line)
        v = [v_ref[at, c, :] for c in range(3)]
        new = collide(table[...], cells_ref[at, 0, :], v, lanes)
        for c in range(3):
            out_ref[c, at, :] = new[c]
        return new

    def add(line, v, lanes):
        return scatter(v, cells_ref[rows_at(line), 1, :], 32, True, lanes)

    sweep(0, v_ref.shape[0] // 8, total, turn, add)
    next_ref[...] = mean_of(total[...])


def leave(
    low, high, v_ref, cells_ref, mean_ref, axis_ref, dir_ref, slot_ref, new_ref, first, moved, table
):
    table[...] = cell_table(mean_ref[...], axis_ref[...])

    def turn(line, lanes):
        at = rows_at(line)
        v = [v_ref[c, at, :] for c in range(3)]
        new = collide(table[...], cells_ref[at, 1, :], v, lanes)
        for c in range(3):
            new_ref[c, rows_at(line - first), :] = new[c]
        return new

    def add(line, v, lanes):
        at = rows_at(line)
        code = dir_ref[at, :]
        key = jnp.where(code > 0, (code - 1) * 256 + slot_ref[at, :], 4096)
        return scatter(v, key, 16, False, lanes)

    sweep(low, high, moved, turn, add)


def part_kernel(low, high, *refs):
    inputs, refs = refs[:6], refs[6:]
    new_ref, moved_ref, table = refs[-3:]
    moved_ref[...] = jnp.zeros_like(moved_ref) if low == 0 else refs[0][...]
    leave(low, high, *inputs, new_ref, low * 8, moved_ref, table)


def places_of(colloid):
    owner = colloid // COLLOIDS_PER_UNIT
    code = jnp.zeros_like(colloid)
    stride = 1
    for axis, up in (("gz", 5), ("gy", 3), ("gx", 1)):
        size = lax.axis_size(axis)
        apart = (owner // stride - lax.axis_index(axis) + size) % size
        code = jnp.where(apart == 1, up, jnp.where(apart == size - 1, up + 1, code))
        stride *= size
    return code * COLLOIDS_PER_UNIT + colloid % COLLOIDS_PER_UNIT


def last_kernel(low, high, *refs):
    inputs, refs = refs[:6], refs[6:]
    before_ref, parts, refs = refs[0], refs[1:3], refs[3:]
    particle_ref, colloid_ref, weight_ref = refs[:3]
    faces = refs[3:5]
    kept_ref, own_ref, *outs = refs[-11:-3]
    moved, table, held = refs[-3:]
    dir_ref = inputs[4]
    moved[...] = before_ref[...]
    start = 0
    for part in parts:
        held[:, start : start + part.shape[1], :] = part[...]
        start += part.shape[1]
    leave(low, high, *inputs, held, 0, moved, table)
    for number, out in enumerate(outs):
        for c in range(3):
            at = 16 * c + 2 * number
            out[2 * c : 2 * c + 2, :] = moved[at : at + 2, :] + moved[48 + at : 50 + at, :]

    def keep(i, carry):
        line = pl.multiple_of(i * 8, 8)
        at = pl.ds(line, 8)
        stays = dir_ref[at, :] == 0
        for c in range(3):
            kept = jnp.where(stays, held[c, at, :], 0.0)
            for j in range(8):
                kept_ref[c : c + 1, pl.ds((line + j) * LANES, LANES)] = kept[j : j + 1]
        return carry

    lines = held.shape[1]
    lax.fori_loop(0, lines // 8, keep, 0, unroll=4)
    high_part, low_part = split(held[...].reshape(3 * lines, LANES))
    wide = jnp.concatenate([high_part, low_part], axis=1).astype(jnp.bfloat16)
    lanes = places(LANES)
    slots = [slice(8 * part, 8 * part + 8) for part in range(particle_ref.shape[0] // 8)]
    terms = []
    for at in slots:
        weight = weight_ref[at, :]
        found = pick(wide, particle_ref[at, :], lines, lanes)
        terms.append([weight * x for x in found] + [weight])
    force = jnp.zeros((128, LANES), jnp.float32)
    for at, values in zip(slots, terms):
        force = force + scatter(values, places_of(colloid_ref[at, :]), 16, False, lanes)
    force = force[0:64] + force[64:128]
    for f in range(4):
        own_ref[2 * f : 2 * f + 2, :] = force[16 * f : 16 * f + 2]
        for number, out in enumerate(outs):
            at = 16 * f + 2 * number + 2
            out[6 + 2 * f : 8 + 2 * f, :] = force[at : at + 2]
    for out, face in zip(outs[4:], faces):
        out[14:15, :] = face[...]


def prepare_kernel(shift_ref, axis_ref, sign_ref, first_ref, last_ref, rise_ref, fall_ref):
    rows = lax.broadcasted_iota(jnp.int32, (8, LANES), 0)
    sign = jnp.zeros((8, LANES), jnp.int32)
    for dim in range(3):
        sign = jnp.where(rows == dim, shift_ref[0, dim], sign)
    sign_ref[...] = sign
    up = jnp.full(rise_ref.shape, shift_ref[0, 0], jnp.int32) > 0
    rise_ref[...] = jnp.where(up, axis_ref[0], axis_ref[1])
    fall_ref[...] = jnp.where(up, axis_ref[1], axis_ref[0])
    first_ref[...] = rise_ref[0 : first_ref.shape[0], :]
    last_ref[...] = fall_ref[fall_ref.shape[0] - last_ref.shape[0] :, :]


def finish_kernel(sign_ref, mean_ref, own_ref, speed_ref, *refs):
    came, (mean_out, moved_out, force_out) = refs[:6], refs[6:]
    mean = mean_ref[...]
    rows = mean.shape[0]
    sides = [jnp.broadcast_to(x[14:15, :], (8, LANES)).T[:rows, 0:1] for x in came[4:]]
    lane = lax.broadcasted_iota(jnp.int32, mean.shape, 1)
    ahead_mean = jnp.where(lane == LANES - 1, sides[1], pltpu.roll(mean, LANES - 1, 1))
    behind_mean = jnp.where(lane == 0, sides[0], pltpu.roll(mean, 1, 1))
    up = jnp.broadcast_to(sign_ref[2:3, :], mean.shape) > 0
    mean_out[...] = jnp.where(up, ahead_mean, behind_mean)
    total = own_ref[...]
    for x in came:
        total = total + x[6:14, :]
    for c in range(3):
        pieces = []
        for x in came:
            pieces += [x[2 * c : 2 * c + 1, :], x[2 * c + 1 : 2 * c + 2, : CAP - LANES]]
        moved_out[c : c + 1, :] = jnp.concatenate(pieces, axis=1)
        for half in range(2):
            at = slice(half * LANES, half * LANES + LANES)
            weight = total[6 + half : 7 + half]
            rest = total[2 * c + half : 2 * c + half + 1] - weight * speed_ref[c : c + 1, at]
            force_out[c : c + 1, at] = rest / jnp.maximum(weight, 1.0)


def call(kernel, name, outs, scratch, flops, args, scalars=0):
    vmem = pl.BlockSpec(memory_space=pltpu.VMEM)
    smem = pl.BlockSpec(memory_space=pltpu.SMEM)
    outs = [out if hasattr(out, "dtype") else jax.ShapeDtypeStruct(out, jnp.float32) for out in outs]
    return pl.pallas_call(
        kernel,
        name=name,
        out_shape=outs,
        in_specs=[smem] * scalars + [vmem] * (len(args) - scalars),
        out_specs=[vmem] * len(outs),
        scratch_shapes=scratch,
        compiler_params=pltpu.CompilerParams(vmem_limit_bytes=VMEM_LIMIT),
        cost_estimate=pl.CostEstimate(flops=flops, bytes_accessed=2 << 20, transcendentals=0),
    )(*args)


def ring(axis, by):
    count = lax.axis_size(axis)
    return [(i, (i + by) % count) for i in range(count)]


def first(x, dim):
    return lax.slice_in_dim(x, 0, 1, axis=dim)


def last(x, dim):
    return lax.slice_in_dim(x, x.shape[dim] - 1, x.shape[dim], axis=dim)


def ahead(x, rim, dim):
    return jnp.concatenate([lax.slice_in_dim(x, 1, x.shape[dim], axis=dim), rim], axis=dim)


def behind(x, rim, dim):
    return jnp.concatenate([rim, lax.slice_in_dim(x, 0, x.shape[dim] - 1, axis=dim)], axis=dim)


def axis_round(rise, fall, sent, dim, axis):
    upper = lax.ppermute(sent[0], axis, ring(axis, -1))
    lower = lax.ppermute(sent[1], axis, ring(axis, 1))
    return ahead(rise, upper, dim), behind(fall, lower, dim), (upper, lower)


def mean_round(mean, up, dim, axis):
    lower = lax.ppermute(last(mean, dim + 1), axis, ring(axis, 1))
    upper = lax.ppermute(first(mean, dim + 1), axis, ring(axis, -1))
    mean = jnp.where(up, ahead(mean, upper, dim + 1), behind(mean, lower, dim + 1))
    return mean, (upper, lower)


def body(
    velocities,
    particle_cells,
    grid_shift,
    axis_index,
    migrate_dir,
    migrate_slot,
    contact_colloid,
    contact_particle,
    contact_weight,
    colloid_velocity,
):
    particles = velocities.shape[1]
    cells_x, cells_y, cells_z = axis_index.shape[1:]
    lines = particles // LANES
    steps = lines // 8
    cuts = (0, steps * 3 // 10, steps * 6 // 10, steps)
    spans = tuple(zip(cuts[:-1], cuts[1:]))
    velocity = velocities.reshape(3, lines, LANES).transpose(1, 0, 2)
    cells = particle_cells.reshape(2, lines, LANES).transpose(1, 0, 2)
    total = pltpu.VMEM((224, LANES), jnp.float32)
    table = pltpu.VMEM((128, 256), jnp.bfloat16)
    pair_flops = 2 * 224 * 128 * particles

    plane, cells_all = cells_y, cells_x * cells_y
    whole = jax.ShapeDtypeStruct((cells_all, cells_z), jnp.int32)
    rim = jax.ShapeDtypeStruct((plane, cells_z), jnp.int32)
    sign, first_rim, last_rim, rise, fall = call(
        prepare_kernel,
        "prepare",
        [jax.ShapeDtypeStruct((8, LANES), jnp.int32), rim, rim, whole, whole],
        [],
        1 << 16,
        (grid_shift, axis_index.reshape(2, cells_all, cells_z)),
        scalars=1,
    )
    up = [sign[dim] > 0 for dim in range(3)]
    rise = rise.reshape(cells_x, cells_y, cells_z)
    fall = fall.reshape(cells_x, cells_y, cells_z)
    sent = (first_rim[None], last_rim[None])
    summed = ()
    for dim, axis in enumerate(("gx", "gy", "gz")):
        rise, fall, rims = axis_round(rise, fall, sent, dim, axis)
        axes = (jnp.where(up[dim], rise, fall), jnp.where(up[dim], fall, rise))
        if dim < 2:
            rise = jnp.where(up[dim + 1], axes[0], axes[1])
            fall = jnp.where(up[dim + 1], axes[1], axes[0])
            sent = (first(rise, dim + 1), last(fall, dim + 1))
        low, high = spans[dim]
        ends = dim == 2
        (result,) = call(
            functools.partial(sum_kernel, low, high, ends),
            "sums_%d" % dim,
            [(96 if ends else 224, LANES)],
            [total],
            pair_flops // 3,
            (velocity, cells) + summed,
        )
        summed = (result,) + rims
    mean0 = result
    axes = [x.reshape(cells_all, cells_z) for x in axes]
    moving, mean1 = call(
        turn_kernel,
        "turn",
        [(3, lines, LANES), (96, LANES)],
        [total, table],
        2 * pair_flops,
        (velocity, cells, mean0, axes[0]),
    )
    shared = (
        moving,
        cells,
        mean1,
        axes[1],
        migrate_dir.reshape(lines, LANES),
        migrate_slot.reshape(lines, LANES),
    )
    mean = mean1.reshape(3, cells_x, cells_y, cells_z)
    tied = ()
    parts = []
    for dim, axis in enumerate(("gx", "gy")):
        mean, rims = mean_round(mean, up[dim], dim, axis)
        low, high = spans[dim]
        part, moved = call(
            functools.partial(part_kernel, low, high),
            "part_%d" % dim,
            [(3, (high - low) * 8, LANES), (96, LANES)],
            [table],
            pair_flops // 2,
            shared + tied,
        )
        parts.append(part)
        tied = (moved,) + rims
    faces = [
        jnp.pad(x.reshape(1, -1), ((0, 0), (0, LANES - 3 * cells_all)))
        for x in (last(mean, 3), first(mean, 3))
    ]
    low, high = spans[2]
    kept, own, *blocks = call(
        functools.partial(last_kernel, low, high),
        "last",
        [(3, particles + 6 * CAP), (8, LANES)] + [(14, LANES)] * 4 + [(15, LANES)] * 2,
        [
            pltpu.VMEM((96, LANES), jnp.float32),
            table,
            pltpu.VMEM((3, lines, LANES), jnp.float32),
        ],
        pair_flops,
        shared
        + (moved, *parts)
        + (
            contact_particle.reshape(-1, LANES),
            contact_colloid.reshape(-1, LANES),
            contact_weight.reshape(-1, LANES),
            *faces,
        )
        + rims,
    )
    came = []
    for number, block in enumerate(blocks):
        axis, by = ("gx", "gy", "gz")[number // 2], 1 - 2 * (number % 2)
        came.append(lax.ppermute(block, axis, ring(axis, by)))
    mean, arrivals, colloid_force = call(
        finish_kernel,
        "finish",
        [(3 * cells_all, cells_z), (3, 6 * CAP), colloid_velocity.shape],
        [],
        1 << 20,
        (sign, mean.reshape(3 * cells_all, cells_z), own, colloid_velocity, *came),
    )
    mean = mean.reshape(3, cells_x, cells_y, cells_z)
    migrated = lax.dynamic_update_slice(kept, arrivals, (0, particles))
    return (mean, migrated, colloid_force)


def solution(mesh):
    flat = P(("gx", "gy", "gz"))
    tall = P(None, ("gx", "gy", "gz"))
    grid = P(None, "gx", "gy", "gz")
    return jax.shard_map(
        body,
        mesh=mesh,
        in_specs=(tall, tall, P(), grid, flat, flat, flat, flat, flat, tall),
        out_specs=(grid, tall, tall),
        check_vma=False,
    )
```

```python
import functools
import math

import jax
import jax.numpy as jnp
from jax import lax
from jax.experimental import pallas as pl
from jax.experimental.pallas import tpu as pltpu
from jax.sharding import PartitionSpec as P

COLLOIDS_PER_UNIT = 256
CAP = 160
LANES = 128
UNROLL = 20
ANGLE = 130.0 * math.pi / 180.0
COS = math.cos(ANGLE)
ALONG = (1.0 - math.cos(ANGLE)) / 3.0
ACROSS = math.sin(ANGLE) / math.sqrt(3.0)
VMEM_LIMIT = 48 << 20


def split(x):
    high = x.astype(jnp.bfloat16).astype(jnp.float32)
    return high, x - high


def places(rows):
    return lax.broadcasted_iota(jnp.int32, (rows, LANES), 0).astype(jnp.float32).astype(jnp.bfloat16)


def narrow(row, rows):
    part = jnp.broadcast_to(row, (16, LANES)).astype(jnp.bfloat16)
    return jnp.concatenate([part] * (rows // 16), axis=0)


def one_hot(row, lanes):
    one, zero = jnp.asarray(1, jnp.bfloat16), jnp.asarray(0, jnp.bfloat16)
    return jnp.where(lanes == narrow(row, LANES), one, zero)


def add_up(left, right):
    return lax.dot_general(
        left, right, (((1,), (1,)), ((), ())), preferred_element_type=jnp.float32
    )


def fold(parts):
    rows = lax.broadcasted_iota(jnp.int32, parts[0].shape, 0)
    step = 1
    while len(parts) > 1:
        low = (rows & step) == 0
        parts = [
            jnp.where(low, p, q) + pltpu.roll(jnp.where(low, q, p), step, 0)
            for p, q in zip(parts[0::2], parts[1::2])
        ]
        step *= 2
    return parts[0]


def rotate(axis, v):
    e = [jnp.where((axis >> bit & 1) == 1, 1.0, -1.0) for bit in range(3)]
    d = (e[0] * v[0] + e[1] * v[1] + e[2] * v[2]) * ALONG
    return [
        COS * v[i]
        + e[i] * d
        + ACROSS * (e[(i + 1) % 3] * v[(i + 2) % 3] - e[(i + 2) % 3] * v[(i + 1) % 3])
        for i in range(3)
    ]


def scatter(values, ids, rows, counted, lanes):
    low = (ids & (LANES - 1)).astype(jnp.float32)
    line = (ids >> 7).astype(jnp.float32)
    parts = [split(x) for x in values]
    parts = [p[0] for p in parts] + [p[1] for p in parts]
    spots = places(rows)
    one, zero = jnp.asarray(1, jnp.bfloat16), jnp.asarray(0, jnp.bfloat16)
    left, right = [], []
    for j in range(8):
        mask = spots == narrow(line[j : j + 1], rows)
        lines = [jnp.where(mask, narrow(x[j : j + 1], rows), zero) for x in parts]
        if counted:
            lines.append(jnp.where(mask, one, zero))
        left.append(jnp.concatenate(lines, axis=0))
        right.append(one_hot(low[j : j + 1], lanes))
    return add_up(jnp.concatenate(left, axis=1), jnp.concatenate(right, axis=1))


def mean_of(total):
    return (total[0:96] + total[96:192]) / jnp.maximum(
        jnp.concatenate([total[192:224]] * 3, axis=0), 1.0
    )


def cell_table(mean, axis):
    m = [mean[32 * i : 32 * i + 32] for i in range(3)]
    turned = rotate(axis, m)
    offset = jnp.concatenate([m[i] - turned[i] for i in range(3)], axis=0)
    high, low = split(offset)
    high = jnp.concatenate([high, axis.astype(jnp.float32)], axis=0)
    low = jnp.concatenate([low, jnp.zeros_like(m[0])], axis=0)
    return jnp.concatenate([high, low], axis=1).astype(jnp.bfloat16)


def pick(table, ids, rows, lanes):
    low = (ids & (LANES - 1)).astype(jnp.float32)
    line = ids >> 7
    spots = lax.broadcasted_iota(jnp.int32, (rows, LANES), 0)
    count = table.shape[0] // rows
    parts = [[] for _ in range(count)]
    for j in range(0, 8, 2):
        hot = jnp.concatenate([one_hot(low[j + k : j + k + 1], lanes) for k in range(2)], axis=1)
        wide = jnp.dot(
            table, jnp.concatenate([hot, hot], axis=0), preferred_element_type=jnp.float32
        )
        for k in range(2):
            mask = spots == jnp.broadcast_to(line[j + k : j + k + 1], (rows, LANES))
            for f in range(count):
                found = jnp.zeros((8, LANES), jnp.float32)
                for row in range(0, rows, 8):
                    at = slice(rows * f + row, rows * f + row + 8)
                    found = jnp.where(
                        mask[row : row + 8], wide[at, k * LANES : (k + 1) * LANES], found
                    )
                parts[f].append(found)
    return [fold(p) for p in parts]


def collide(table, cells, v, lanes):
    picked = pick(table, cells, 32, lanes)
    turned = rotate(picked[3].astype(jnp.int32), v)
    return [turned[i] + picked[i] for i in range(3)]


def sweep(low, high, total, pick_block, add_block):
    count = high - low
    unroll = max(u for u in range(1, UNROLL + 1) if count % u == 0)

    def step(i, carry):
        lanes = places(LANES)
        added, held = 0.0, None
        for part in range(unroll + 1):
            line = pl.multiple_of((low + i * unroll + part) * 8, 8)
            new = pick_block(line, lanes) if part < unroll else None
            if part:
                added += add_block(line - 8, held, lanes)
            held = new
        total[...] += added
        return carry

    lax.fori_loop(0, count // unroll, step, 0)


def rows_at(line):
    return pl.ds(pl.multiple_of(line, 8), 8)


def sum_kernel(low, high, ends, v_ref, cells_ref, *refs):
    out_ref, total = refs[-2:]
    total[...] = jnp.zeros_like(total) if low == 0 else refs[0][...]

    def load(line, lanes):
        return [v_ref[rows_at(line), c, :] for c in range(3)]

    def add(line, v, lanes):
        return scatter(v, cells_ref[rows_at(line), 0, :], 32, True, lanes)

    sweep(low, high, total, load, add)
    out_ref[...] = mean_of(total[...]) if ends else total[...]


def turn_kernel(v_ref, cells_ref, mean_ref, axis_ref, out_ref, next_ref, total, table):
    total[...] = jnp.zeros_like(total)
    table[...] = cell_table(mean_ref[...], axis_ref[...])

    def turn(line, lanes):
        at = rows_at(line)
        v = [v_ref[at, c, :] for c in range(3)]
        new = collide(table[...], cells_ref[at, 0, :], v, lanes)
        for c in range(3):
            out_ref[c, at, :] = new[c]
        return new

    def add(line, v, lanes):
        return scatter(v, cells_ref[rows_at(line), 1, :], 32, True, lanes)

    sweep(0, v_ref.shape[0] // 8, total, turn, add)
    next_ref[...] = mean_of(total[...])


def leave(
    low, high, v_ref, cells_ref, mean_ref, axis_ref, dir_ref, slot_ref, new_ref, first, moved, table
):
    table[...] = cell_table(mean_ref[...], axis_ref[...])

    def turn(line, lanes):
        at = rows_at(line)
        v = [v_ref[c, at, :] for c in range(3)]
        new = collide(table[...], cells_ref[at, 1, :], v, lanes)
        for c in range(3):
            new_ref[c, rows_at(line - first), :] = new[c]
        return new

    def add(line, v, lanes):
        at = rows_at(line)
        code = dir_ref[at, :]
        key = jnp.where(code > 0, (code - 1) * 256 + slot_ref[at, :], 4096)
        return scatter(v, key, 16, False, lanes)

    sweep(low, high, moved, turn, add)


def part_kernel(low, high, *refs):
    inputs, refs = refs[:6], refs[6:]
    new_ref, moved_ref, table = refs[-3:]
    moved_ref[...] = jnp.zeros_like(moved_ref) if low == 0 else refs[0][...]
    leave(low, high, *inputs, new_ref, low * 8, moved_ref, table)


def places_of(colloid):
    owner = colloid // COLLOIDS_PER_UNIT
    code = jnp.zeros_like(colloid)
    stride = 1
    for axis, up in (("gz", 5), ("gy", 3), ("gx", 1)):
        size = lax.axis_size(axis)
        apart = (owner // stride - lax.axis_index(axis) + size) % size
        code = jnp.where(apart == 1, up, jnp.where(apart == size - 1, up + 1, code))
        stride *= size
    return code * COLLOIDS_PER_UNIT + colloid % COLLOIDS_PER_UNIT


def last_kernel(low, high, *refs):
    inputs, refs = refs[:6], refs[6:]
    before_ref, parts, refs = refs[0], refs[1:2], refs[2:]
    particle_ref, colloid_ref, weight_ref = refs[:3]
    kept_ref, own_ref, *outs = refs[-11:-3]
    moved, table, held = refs[-3:]
    dir_ref = inputs[4]
    moved[...] = before_ref[...]
    start = 0
    for part in parts:
        held[:, start : start + part.shape[1], :] = part[...]
        start += part.shape[1]
    leave(low, high, *inputs, held, 0, moved, table)
    for number, out in enumerate(outs):
        for c in range(3):
            at = 16 * c + 2 * number
            out[2 * c : 2 * c + 2, :] = moved[at : at + 2, :] + moved[48 + at : 50 + at, :]

    def keep(i, carry):
        line = pl.multiple_of(i * 8, 8)
        at = pl.ds(line, 8)
        stays = dir_ref[at, :] == 0
        for c in range(3):
            kept = jnp.where(stays, held[c, at, :], 0.0)
            for j in range(8):
                kept_ref[c : c + 1, pl.ds((line + j) * LANES, LANES)] = kept[j : j + 1]
        return carry

    lines = held.shape[1]
    lax.fori_loop(0, lines // 8, keep, 0, unroll=4)
    high_part, low_part = split(held[...].reshape(3 * lines, LANES))
    wide = jnp.concatenate([high_part, low_part], axis=1).astype(jnp.bfloat16)
    lanes = places(LANES)
    slots = [slice(8 * part, 8 * part + 8) for part in range(particle_ref.shape[0] // 8)]
    terms = []
    for at in slots:
        weight = weight_ref[at, :]
        found = pick(wide, particle_ref[at, :], lines, lanes)
        terms.append([weight * x for x in found] + [weight])
    force = jnp.zeros((128, LANES), jnp.float32)
    for at, values in zip(slots, terms):
        force = force + scatter(values, places_of(colloid_ref[at, :]), 16, False, lanes)
    force = force[0:64] + force[64:128]
    for f in range(4):
        own_ref[2 * f : 2 * f + 2, :] = force[16 * f : 16 * f + 2]
        for number, out in enumerate(outs):
            at = 16 * f + 2 * number + 2
            out[6 + 2 * f : 8 + 2 * f, :] = force[at : at + 2]
    for out in outs:
        out[14:16, :] = jnp.zeros((2, LANES), jnp.float32)


def prepare_kernel(all_ref, sign_ref, first_ref, last_ref, rise_ref, fall_ref):
    rows = rise_ref.shape[0]
    sign_ref[...] = all_ref[2 * rows :, :]
    up = jnp.broadcast_to(all_ref[2 * rows : 2 * rows + 1, :], rise_ref.shape) > 0
    axes = [all_ref[0:rows, :], all_ref[rows : 2 * rows, :]]
    rise_ref[...] = jnp.where(up, axes[0], axes[1])
    fall_ref[...] = jnp.where(up, axes[1], axes[0])
    first_ref[...] = rise_ref[0 : first_ref.shape[0], :]
    last_ref[...] = fall_ref[fall_ref.shape[0] - last_ref.shape[0] :, :]


def finish_kernel(sign_ref, mean_ref, own_ref, speed_ref, *refs):
    came, (mean_out, moved_out, force_out) = refs[:6], refs[6:]
    mean = mean_ref[...]
    rows = mean.shape[0]
    sides = [jnp.broadcast_to(x[16:17, :], (8, LANES)).T[:rows, 0:1] for x in came[4:]]
    lane = lax.broadcasted_iota(jnp.int32, mean.shape, 1)
    ahead_mean = jnp.where(lane == LANES - 1, sides[1], pltpu.roll(mean, LANES - 1, 1))
    behind_mean = jnp.where(lane == 0, sides[0], pltpu.roll(mean, 1, 1))
    up = jnp.broadcast_to(sign_ref[2:3, :], mean.shape) > 0
    mean_out[...] = jnp.where(up, ahead_mean, behind_mean)
    total = own_ref[...]
    for x in came:
        total = total + x[6:14, :]
    for c in range(3):
        pieces = []
        for x in came:
            pieces += [x[2 * c : 2 * c + 1, :], x[2 * c + 1 : 2 * c + 2, : CAP - LANES]]
        moved_out[c : c + 1, :] = jnp.concatenate(pieces, axis=1)
        for half in range(2):
            at = slice(half * LANES, half * LANES + LANES)
            weight = total[6 + half : 7 + half]
            rest = total[2 * c + half : 2 * c + half + 1] - weight * speed_ref[c : c + 1, at]
            force_out[c : c + 1, at] = rest / jnp.maximum(weight, 1.0)


def call(kernel, name, outs, scratch, flops, args):
    vmem = pl.BlockSpec(memory_space=pltpu.VMEM)
    outs = [out if hasattr(out, "dtype") else jax.ShapeDtypeStruct(out, jnp.float32) for out in outs]
    return pl.pallas_call(
        kernel,
        name=name,
        out_shape=outs,
        in_specs=[vmem] * len(args),
        out_specs=[vmem] * len(outs),
        scratch_shapes=scratch,
        compiler_params=pltpu.CompilerParams(vmem_limit_bytes=VMEM_LIMIT),
        cost_estimate=pl.CostEstimate(flops=flops, bytes_accessed=2 << 20, transcendentals=0),
    )(*args)


def ring(axis, by):
    count = lax.axis_size(axis)
    return [(i, (i + by) % count) for i in range(count)]


def first(x, dim):
    return lax.slice_in_dim(x, 0, 1, axis=dim)


def last(x, dim):
    return lax.slice_in_dim(x, x.shape[dim] - 1, x.shape[dim], axis=dim)


def ahead(x, rim, dim):
    return jnp.concatenate([lax.slice_in_dim(x, 1, x.shape[dim], axis=dim), rim], axis=dim)


def behind(x, rim, dim):
    return jnp.concatenate([rim, lax.slice_in_dim(x, 0, x.shape[dim] - 1, axis=dim)], axis=dim)


def axis_round(rise, fall, sent, dim, axis):
    upper = lax.ppermute(sent[0], axis, ring(axis, -1))
    lower = lax.ppermute(sent[1], axis, ring(axis, 1))
    return ahead(rise, upper, dim), behind(fall, lower, dim), (upper, lower)


def mean_round(mean, up, dim, axis):
    lower = lax.ppermute(last(mean, dim + 1), axis, ring(axis, 1))
    upper = lax.ppermute(first(mean, dim + 1), axis, ring(axis, -1))
    mean = jnp.where(up, ahead(mean, upper, dim + 1), behind(mean, lower, dim + 1))
    return mean, (upper, lower)


def body(
    velocities,
    particle_cells,
    grid_shift,
    axis_index,
    migrate_dir,
    migrate_slot,
    contact_colloid,
    contact_particle,
    contact_weight,
    colloid_velocity,
):
    particles = velocities.shape[1]
    cells_x, cells_y, cells_z = axis_index.shape[1:]
    lines = particles // LANES
    steps = lines // 8
    cuts = (0, steps * 3 // 10, steps * 6 // 10, steps)
    spans = tuple(zip(cuts[:-1], cuts[1:]))
    velocity = velocities.reshape(3, lines, LANES).transpose(1, 0, 2)
    cells = particle_cells.reshape(2, lines, LANES).transpose(1, 0, 2)
    total = pltpu.VMEM((224, LANES), jnp.float32)
    table = pltpu.VMEM((128, 256), jnp.bfloat16)
    pair_flops = 2 * 224 * 128 * particles

    plane, cells_all = cells_y, cells_x * cells_y
    whole = jax.ShapeDtypeStruct((cells_all, cells_z), jnp.int32)
    rim = jax.ShapeDtypeStruct((plane, cells_z), jnp.int32)
    shifts = jnp.broadcast_to(jnp.pad(grid_shift[0], (0, 5))[:, None], (8, LANES))
    sign, first_rim, last_rim, rise, fall = call(
        prepare_kernel,
        "prepare",
        [jax.ShapeDtypeStruct((8, LANES), jnp.int32), rim, rim, whole, whole],
        [],
        1 << 16,
        (jnp.concatenate([axis_index.reshape(2 * cells_all, cells_z), shifts], axis=0),),
    )
    up = [sign[dim] > 0 for dim in range(3)]
    rise = rise.reshape(cells_x, cells_y, cells_z)
    fall = fall.reshape(cells_x, cells_y, cells_z)
    sent = (first_rim[None], last_rim[None])
    summed = ()
    for dim, axis in enumerate(("gx", "gy", "gz")):
        rise, fall, rims = axis_round(rise, fall, sent, dim, axis)
        axes = (jnp.where(up[dim], rise, fall), jnp.where(up[dim], fall, rise))
        if dim < 2:
            rise = jnp.where(up[dim + 1], axes[0], axes[1])
            fall = jnp.where(up[dim + 1], axes[1], axes[0])
            sent = (first(rise, dim + 1), last(fall, dim + 1))
        low, high = spans[dim]
        ends = dim == 2
        (result,) = call(
            functools.partial(sum_kernel, low, high, ends),
            "sums_%d" % dim,
            [(96 if ends else 224, LANES)],
            [total],
            pair_flops // 3,
            (velocity, cells) + summed,
        )
        summed = (result,) + rims
    mean0 = result
    axes = [x.reshape(cells_all, cells_z) for x in axes]
    moving, mean1 = call(
        turn_kernel,
        "turn",
        [(3, lines, LANES), (96, LANES)],
        [total, table],
        2 * pair_flops,
        (velocity, cells, mean0, axes[0]),
    )
    shared = (
        moving,
        cells,
        mean1,
        axes[1],
        migrate_dir.reshape(lines, LANES),
        migrate_slot.reshape(lines, LANES),
    )
    mean = mean1.reshape(3, cells_x, cells_y, cells_z)
    tied = ()
    parts = []
    for dim, axis in enumerate(("gx",)):
        mean, rims = mean_round(mean, up[dim], dim, axis)
        low, high = 0, steps // 2
        part, moved = call(
            functools.partial(part_kernel, low, high),
            "part_%d" % dim,
            [(3, (high - low) * 8, LANES), (96, LANES)],
            [table],
            pair_flops // 2,
            shared + tied,
        )
        parts.append(part)
        tied = (moved,) + rims
    low, high = steps // 2, steps
    kept, own, *blocks = call(
        functools.partial(last_kernel, low, high),
        "last",
        [(3, particles + 6 * CAP), (8, LANES)] + [(16, LANES)] * 6,
        [
            pltpu.VMEM((96, LANES), jnp.float32),
            table,
            pltpu.VMEM((3, lines, LANES), jnp.float32),
        ],
        pair_flops,
        shared
        + (moved, *parts)
        + (
            contact_particle.reshape(-1, LANES),
            contact_colloid.reshape(-1, LANES),
            contact_weight.reshape(-1, LANES),
        )
        + rims,
    )
    came = []
    for dim, axis in enumerate(("gx", "gy", "gz")):
        rims = []
        for side, cut in enumerate((last, first)):
            sent = blocks[2 * dim + side]
            if dim:
                rim = cut(mean, dim + 1)
                shape = rim.shape
                if dim == 2:
                    rim = jnp.pad(rim.reshape(1, -1), ((0, 0), (0, LANES - 3 * cells_all)))
                sent = jnp.concatenate([sent, rim.reshape(-1, LANES)], axis=0)
            came.append(lax.ppermute(sent, axis, ring(axis, 1 - 2 * side)))
            rims.append(came[-1][16:])
        if dim == 1:
            lower, upper = [x.reshape(shape) for x in rims]
            mean = jnp.where(up[dim], ahead(mean, upper, dim + 1), behind(mean, lower, dim + 1))
    mean, arrivals, colloid_force = call(
        finish_kernel,
        "finish",
        [(3 * cells_all, cells_z), (3, 6 * CAP), colloid_velocity.shape],
        [],
        1 << 20,
        (sign, mean.reshape(3 * cells_all, cells_z), own, colloid_velocity, *came),
    )
    mean = mean.reshape(3, cells_x, cells_y, cells_z)
    migrated = lax.dynamic_update_slice(kept, arrivals, (0, particles))
    return (mean, migrated, colloid_force)


def solution(mesh):
    flat = P(("gx", "gy", "gz"))
    tall = P(None, ("gx", "gy", "gz"))
    grid = P(None, "gx", "gy", "gz")
    return jax.shard_map(
        body,
        mesh=mesh,
        in_specs=(tall, tall, P(), grid, flat, flat, flat, flat, flat, tall),
        out_specs=(grid, tall, tall),
        check_vma=False,
    )
```
